256 devices in a mesh: dp: 2 (over y_lo), fsdp: 16 (over z, y_hi), seq: 8 (over x, core).
Axes of the slice: x: 4, y: 4 (y_hi: 2, y_lo: 2; y = y_hi * 2 + y_lo), z: 8, core: 2. Of those that a mesh axis runs over, the one named last changes fastest.
Arguments:
- latents: bfloat16 [32, 512, 2, 3072], P(('dp', 'fsdp'), 'seq'), may hold values from -6 to 6
- noise: bfloat16 [32, 512, 2, 3072], P(('dp', 'fsdp'), 'seq'), may hold values from -12 to 12
- timesteps: int32 [32, 2], P(('dp', 'fsdp')), may hold values from 0 to 999
- ref_errors: float32 [32, 2], P(('dp', 'fsdp')), may hold values from 1.5 to 2.5
- norm_gain: float32 [3072], replicated, may hold values from 0.25 to 1.75
- w_query: bfloat16 [3072, 2048], P('fsdp', 'seq'), as said below
- w_key: bfloat16 [3072, 2048], P('fsdp', 'seq'), as said below
- w_value: bfloat16 [3072, 2048], P('fsdp', 'seq'), may hold values from -0.109375 to 0.109375
- w_out: bfloat16 [2048, 3072], P('seq', 'fsdp'), may hold values from -0.125 to 0.125
Outputs:
- grad_value: bfloat16 [3072, 2048], P(('dp', 'fsdp'), 'seq')
- grad_out: bfloat16 [2048, 3072], P('seq', ('dp', 'fsdp'))
- pair_loss: float32 [32], P(('dp', 'fsdp'))
The draws below stay inside these ranges and needn't reach their ends.
Inputs may be any that keep to these rules, and one draw needn't show every extreme that they name: `w_query`: columns of the query projection, of order 1 / sqrt(3072). `w_key`: columns of the key projection.
All inputs are finite; a program needn't handle non-finite values.
Results may differ from the reference program's by a relative error of at most 0.025.
Values may be sent and summed in bfloat16 or wider, within the bound.
No kernel may reach another device: no remote copies, remote signals or barrier semaphores. Data moves between devices by JAX's collectives and lax.ppermute only.
A program may use at most 128 MiB of HBM per device.

```python
import math
import jax
import jax.numpy as jnp
from jax import lax

D = 3072
HD = 128
HEADS = 16
LEN = 512
NSTEP = 1000
PAIRS = 32
LOSS_SCALE = 24576
N_SEQ = 8


def shared_weight(key):
    return jnp.clip(jax.random.normal(key, (D, HEADS * HD), jnp.float32), -5.0, 5.0) / math.sqrt(D)


def draw_w_query(key, part):
    base = shared_weight(key)
    return base.astype(jnp.bfloat16)


def draw_w_key(key, part):
    key = jax.random.fold_in(key, 12)
    return (jnp.clip(jax.random.normal(key, (D, HEADS * HD), jnp.float32), -5.0, 5.0) / math.sqrt(D)).astype(jnp.bfloat16)


def token_profile(ratio):
    position = jnp.arange(LEN, dtype=jnp.float32) / (LEN - 1) - 0.5
    rising = jnp.exp(math.log(ratio) * position)
    return jnp.stack([rising, 1.0 / rising], axis=1)[None, :, :, None]


def draw_noise(key, part):
    key = jax.random.fold_in(key, 13)
    values = jnp.clip(jax.random.normal(key, (PAIRS, LEN, 2, D), jnp.float32), -5.0, 5.0)
    return (values * token_profile(3.0)).astype(jnp.bfloat16)


def place_ends(result, key, low, top_value):
    spot = [jax.random.randint(jax.random.fold_in(key, axis), (), 0, length) for axis, length in enumerate(result.shape)]
    main_axis = result.shape.index(max(result.shape))
    neighbour = spot[:main_axis] + [(spot[main_axis] + 1) % result.shape[main_axis]] + spot[main_axis + 1:]
    return result.at[tuple(spot)].set(low).at[tuple(neighbour)].set(top_value)


def level_of(stream_key, extent, shards, smallest, high):
    def one(dim, shards_of):
        steps = jax.random.uniform(jax.random.fold_in(jax.random.fold_in(stream_key, 6), dim), (shards_of,), jnp.float32, smallest / len(shards), high / len(shards))
        return jnp.repeat(jnp.exp(steps), extent[dim] // shards_of).reshape((-1,) + (1,) * (len(extent) - dim - 1))

    factor_of = one(*shards[0])
    for cut in shards[1:]:
        factor_of = factor_of * one(*cut)
    return factor_of


def bell_draw(own_key, dims, scale, most, shards=(), kind=jnp.bfloat16):
    drawn = jax.random.normal(own_key, dims, jnp.float32) * scale
    if len(shards) > 0:
        drawn = level_of(own_key, dims, shards, -0.22, 0.18) * drawn
    return jnp.clip(drawn, min=-most, max=most).astype(kind)


def setup_inputs(seed: int = 0) -> dict:
    streams_of = jax.random.split(jax.random.key(seed), 10)
    latents = bell_draw(streams_of[0], (PAIRS, LEN, 2, D), 1.0, 6.0, ((0, 32), (1, 8)))
    noise = draw_noise(jax.random.fold_in(streams_of[9], 71), 0)
    timesteps = place_ends(jax.random.randint(streams_of[2], (PAIRS, 2), 0, NSTEP), jax.random.fold_in(streams_of[2], 1), 0, NSTEP - 1).astype(jnp.int32)
    ref_errors = jnp.clip(1.5 + 1.0 * jax.random.uniform(streams_of[3], (PAIRS, 2), jnp.float32) ** level_of(streams_of[3], (PAIRS, 2), ((0, 32),), -0.2, 0.2), 1.5, 2.5)
    norm_gain = jnp.clip(1.0 + 0.15 * jax.random.normal(streams_of[4], (D,), jnp.float32), 0.25, 1.75)
    w_query = draw_w_query(jax.random.fold_in(streams_of[9], 71), 0)
    w_key = draw_w_key(jax.random.fold_in(streams_of[9], 71), 0)
    w_value = bell_draw(streams_of[7], (D, HEADS * HD), D ** -0.5, 0.109375, ((0, 16), (1, 8)))
    w_out = bell_draw(streams_of[8], (HEADS * HD, D), (HEADS * HD) ** -0.5, 0.125, ((0, 8), (1, 16)))
    return dict(latents=latents, noise=noise, timesteps=timesteps, ref_errors=ref_errors, norm_gain=norm_gain, w_query=w_query, w_key=w_key, w_value=w_value, w_out=w_out)


preference_beta = 2.0
norm_epsilon = 1e-06

def rms_normed(values, norm_gain):
    values = values.astype(jnp.float32)
    inverse = lax.rsqrt(lax.optimization_barrier(jnp.mean(values * values, axis=-1, keepdims=True)) + norm_epsilon)
    return (values * inverse * norm_gain.astype(jnp.float32)).astype(jnp.bfloat16)

def reference(latents, noise, timesteps, ref_errors, norm_gain, w_query, w_key, w_value, w_out):
    width = HEADS * HD
    group_width = width // N_SEQ

    def one_pair(carry, inputs):
        grad_val, grad_outt = carry
        clean, noise_pair, steps_pair, ref_pair = inputs
        sigma = (steps_pair.astype(jnp.float32) + 0.5) / NSTEP
        mixing = sigma[None, :, None]
        clean32 = clean.astype(jnp.float32)
        noise32 = noise_pair.astype(jnp.float32)
        noised = ((1.0 - mixing) * clean32 + mixing * noise32).astype(jnp.bfloat16)
        target = noise32 - clean32
        normed = rms_normed(noised, norm_gain)
        rows = normed.reshape(LEN * 2, D)

        def project(weight):
            return jnp.dot(rows, weight, preferred_element_type=jnp.float32).astype(jnp.bfloat16).reshape(LEN, 2, HEADS, HD)
        query = project(w_query)
        keys = project(w_key)
        values = project(w_value)
        scores = jnp.einsum('tihd,sihd->ihts', query.astype(jnp.float32), keys.astype(jnp.float32)) / math.sqrt(HD)
        probs = jax.nn.softmax(scores, axis=-1).astype(jnp.bfloat16)
        attended = jnp.einsum('ihts,sihd->tihd', probs.astype(jnp.float32), values.astype(jnp.float32)).astype(jnp.bfloat16)
        attended = attended.reshape(LEN * 2, width)
        grouped = attended.reshape(LEN * 2, N_SEQ, group_width).astype(jnp.float32)
        out_groups = w_out.reshape(N_SEQ, group_width, D).astype(jnp.float32)
        partial_terms = jnp.einsum('rgc,gcd->grd', grouped, out_groups).astype(jnp.bfloat16)
        partial_terms = lax.optimization_barrier(partial_terms)
        predicted = lax.optimization_barrier(jnp.sum(partial_terms.astype(jnp.float32), axis=0)).reshape(LEN, 2, D)
        differ = predicted - target
        errors = lax.optimization_barrier(jnp.mean(differ * differ, axis=(0, 2)))
        residual = differ.astype(jnp.bfloat16)
        margin = errors[0] - ref_pair[0] - (errors[1] - ref_pair[1])
        pair_loss = jax.nn.softplus(preference_beta * margin)
        weight_pair = preference_beta * jax.nn.sigmoid(preference_beta * margin) * 2.0 * LOSS_SCALE / (LEN * D)
        image_scale = jnp.array([1.0, -1.0], jnp.float32) * weight_pair
        attended3 = attended.reshape(LEN, 2, width)
        out_terms = jnp.einsum('tid,tic->idc', residual.astype(jnp.float32), attended3.astype(jnp.float32))
        grad_outt = grad_outt + lax.optimization_barrier(jnp.sum(out_terms * image_scale[:, None, None], axis=0))
        d_attended = jnp.dot(residual.reshape(LEN * 2, D), w_out.T, preferred_element_type=jnp.float32)
        d_attended = (d_attended.reshape(LEN, 2, width) * image_scale[None, :, None]).astype(jnp.bfloat16)
        d_attended = d_attended.reshape(LEN, 2, HEADS, HD)
        d_values = jnp.einsum('ihts,tihd->sihd', probs.astype(jnp.float32), d_attended.astype(jnp.float32)).astype(jnp.bfloat16)
        d_values = d_values.reshape(LEN * 2, width)
        grad_val = grad_val + jnp.dot(rows.T, d_values, preferred_element_type=jnp.float32)
        return ((grad_val, grad_outt), pair_loss)
    start = (jnp.zeros((D, width), jnp.float32), jnp.zeros((D, width), jnp.float32))
    (grad_val, grad_outt), losses = lax.scan(one_pair, start, (latents, noise, timesteps, ref_errors))
    return (grad_val.astype(jnp.bfloat16), grad_outt.T.astype(jnp.bfloat16), losses)
```

```python
import math

import jax
import jax.numpy as jnp
from jax import lax
from jax.sharding import Mesh, PartitionSpec as P

HD = 128
NSTEP = 1000
LOSS_SCALE = 24576
NZ = 8

preference_beta = 2.0
norm_epsilon = 1e-06

SEQ = ("x", "core")
GROUP = ("dp", "z", "yh")
Y = ("dp", "yh")
bf16 = jnp.bfloat16
f32 = jnp.float32


def shift(value, axis, step, count):
    return lax.ppermute(value, axis, [(i, (i + step) % count) for i in range(count)])


def flip(value, axis, mask, count):
    return lax.ppermute(value, axis, [(i, i ^ mask) for i in range(count)])


def gather_weight(mine, other, y_hi):
    crossed = flip(other, Y, 3, 4)
    first = jnp.where(y_hi == 0, jnp.stack([mine, crossed]), jnp.stack([crossed, mine]))

    def hand_over(blocks):
        low = flip(jnp.stack([block[0] for block in blocks]), Y, 2, 4)
        high = flip(jnp.stack([block[1] for block in blocks]), Y, 3, 4)
        return [(low[i], high[i]) for i in range(len(blocks))]

    held = {0: first}
    given = {}
    right = left = first
    for step in range(1, 4):
        right = shift(right, "z", 1, NZ)
        left = shift(left, "z", NZ - 1, NZ)
        held[NZ - step] = right
        held[step] = left
        keys = [0, NZ - 1, 1] if step == 1 else [NZ - step, step]
        for key, value in zip(keys, hand_over([held[k] for k in keys])):
            given[key] = value
    far_low = shift(right[0], "z", 1, NZ)
    far_high = shift(left[1], "z", NZ - 1, NZ)
    held[4] = (far_low, far_high)
    given[4] = (flip(far_low, Y, 2, 4), flip(far_high, Y, 3, 4))
    own = jnp.concatenate([part for k in range(NZ) for part in (held[k][0], held[k][1])], axis=0)
    rest = jnp.concatenate([part for k in range(NZ) for part in given[k]], axis=0)
    return own, rest


def reduce_gradient(grad, dp, z, y_hi):
    pieces = grad.astype(bf16).reshape(2, NZ, 2, -1, grad.shape[1])
    total = None
    for mask in range(4):
        piece = lax.dynamic_index_in_dim(pieces, dp ^ (mask >> 1), 0, keepdims=False)
        piece = lax.dynamic_index_in_dim(piece, y_hi ^ (mask & 1), 1, keepdims=False)
        term = (piece if mask == 0 else flip(piece, Y, mask, 4)).astype(f32)
        total = term if total is None else total + term
    shares = total.astype(bf16)
    result = None
    for step in range(NZ):
        piece = lax.dynamic_index_in_dim(shares, (z + step) % NZ, 0, keepdims=False)
        term = (piece if step == 0 else shift(piece, "z", step, NZ)).astype(f32)
        result = term if result is None else result + term
    return result.astype(bf16)


def body(latents, noise, timesteps, ref_errors, norm_gain, w_query, w_key, w_value, w_out):
    dp, z, y_hi = lax.axis_index("dp"), lax.axis_index("z"), lax.axis_index("yh")
    local_len, model_width = latents.shape[1], latents.shape[3]
    full_len = local_len * 8
    rows_count = 2 * full_len
    z_rows = model_width // NZ

    def rolled(value, offset, axis):
        twice = jnp.concatenate([value, value], axis=axis)
        return lax.dynamic_slice_in_dim(twice, offset * z_rows, model_width, axis)

    def head(weight, which):
        return jnp.where(which == 0, weight[:, :HD], weight[:, HD:])

    def heads(which):
        return jnp.concatenate([head(w, which) for w in (w_query, w_key, w_value)], axis=1)

    w_out_t = w_out.T
    qkv_w = gather_weight(heads(dp), heads(1 - dp), y_hi)
    out_w = gather_weight(head(w_out_t, dp), head(w_out_t, 1 - dp), y_hi)
    out_w = jnp.concatenate(out_w, axis=1)

    clean32 = rolled(latents[0], z, 2).transpose(1, 0, 2).astype(f32)
    noise32 = rolled(noise[0], z, 2).transpose(1, 0, 2).astype(f32)
    gain = rolled(norm_gain, z, 0)
    sigma = (timesteps[0].astype(f32) + 0.5) / NSTEP
    mixing = sigma[:, None, None]
    noised = ((1.0 - mixing) * clean32 + mixing * noise32).astype(bf16).astype(f32)
    target = noise32 - clean32
    inverse = lax.rsqrt(jnp.mean(noised * noised, axis=-1, keepdims=True) + norm_epsilon)
    normed = (noised * inverse * gain).astype(bf16)
    normed = lax.all_gather(normed, SEQ, axis=1, tiled=True)
    rows = normed.reshape(rows_count, model_width)

    attended, probs = [], []
    for weight in qkv_w:
        qkv = jnp.dot(rows, weight, preferred_element_type=f32).astype(bf16)
        qkv = qkv.reshape(2, full_len, 3 * HD)
        query, keys, values = qkv[..., :HD], qkv[..., HD : 2 * HD], qkv[..., 2 * HD :]
        scores = jnp.einsum("ith,ish->its", query, keys, preferred_element_type=f32) / math.sqrt(HD)
        prob = jax.nn.softmax(scores, axis=-1).astype(bf16)
        probs.append(prob)
        attended.append(
            jnp.einsum("its,ish->ith", prob, values, preferred_element_type=f32).astype(bf16)
        )
    attended = jnp.concatenate(attended, axis=2)
    partial = lax.dot_general(
        attended.reshape(rows_count, 2 * HD),
        out_w,
        (((1,), (1,)), ((), ())),
        preferred_element_type=f32,
    ).astype(bf16)
    predicted = lax.psum_scatter(
        partial.reshape(2, full_len, model_width), SEQ, scatter_dimension=1, tiled=True
    ).astype(f32)
    differ = predicted - target
    residual = lax.all_gather(differ.astype(bf16), SEQ, axis=1, tiled=True)
    sums = jnp.sum(differ * differ, axis=(1, 2))
    sums = sums + flip(sums, "core", 1, 2)
    sums = sums + flip(sums, "x", 1, 4)
    sums = sums + flip(sums, "x", 2, 4)
    errors = sums / (full_len * model_width)
    reference_pair = ref_errors[0]
    margin = errors[0] - reference_pair[0] - (errors[1] - reference_pair[1])
    pair_loss = jax.nn.softplus(preference_beta * margin)
    weight_pair = (
        preference_beta
        * jax.nn.sigmoid(preference_beta * margin)
        * 2.0
        * LOSS_SCALE
        / (full_len * model_width)
    )
    image_scale = jnp.array([1.0, -1.0], f32) * weight_pair

    def placed(grad):
        grad = rolled(grad, (NZ - z) % NZ, 0)
        return jnp.where(dp == 0, grad, jnp.concatenate([grad[:, HD:], grad[:, :HD]], axis=1))

    per_image = lax.dot_general(
        residual, attended, (((1,), (1,)), ((0,), (0,))), preferred_element_type=f32
    )
    grad_out = jnp.sum(per_image * image_scale[:, None, None], axis=0)
    grad_out = reduce_gradient(placed(grad_out.astype(bf16)), dp, z, y_hi)
    d_attended = jnp.dot(
        residual.reshape(rows_count, model_width), out_w, preferred_element_type=f32
    )
    d_attended = d_attended.reshape(2, full_len, 2 * HD) * image_scale[:, None, None]
    d_attended = d_attended.astype(bf16)
    d_values = jnp.concatenate(
        [
            jnp.einsum(
                "its,ith->ish", probs[e], d_attended[..., e * HD : (e + 1) * HD],
                preferred_element_type=f32,
            ).astype(bf16)
            for e in range(2)
        ],
        axis=2,
    )
    grad_value = lax.dot_general(
        rows, d_values.reshape(rows_count, 2 * HD), (((0,), (0,)), ((), ())),
        preferred_element_type=f32,
    )
    grad_value = reduce_gradient(placed(grad_value.astype(bf16)), dp, z, y_hi)
    return grad_value, grad_out.T, pair_loss.reshape(1)


def solution(mesh):
    fine = Mesh(mesh.devices.reshape(2, NZ, 2, 4, 2), ("dp", "z", "yh", "x", "core"))
    fsdp = ("z", "yh")
    in_specs = (
        P(GROUP, SEQ, None, None),
        P(GROUP, SEQ, None, None),
        P(GROUP, None),
        P(GROUP, None),
        P(),
        P(fsdp, SEQ),
        P(fsdp, SEQ),
        P(fsdp, SEQ),
        P(SEQ, fsdp),
    )
    out_specs = (P(GROUP, SEQ), P(SEQ, GROUP), P(GROUP))
    return jax.shard_map(body, mesh=fine, in_specs=in_specs, out_specs=out_specs, check_vma=False)
```

```python
import functools
import math

import jax
import jax.numpy as jnp
from jax import lax
from jax.experimental import pallas as pl
from jax.experimental.pallas import tpu as pltpu
from jax.sharding import Mesh, PartitionSpec as P

HD = 128
NSTEP = 1000
LOSS_SCALE = 24576
NZ = 8

preference_beta = 2.0
norm_epsilon = 1e-06

SEQ = ("x", "core")
GROUP = ("dp", "z", "yh")
Y = ("dp", "yh")
bf16 = jnp.bfloat16
f32 = jnp.float32


def shift(value, axis, step, count):
    return lax.ppermute(value, axis, [(i, (i + step) % count) for i in range(count)])


def flip(value, axis, mask, count):
    return lax.ppermute(value, axis, [(i, i ^ mask) for i in range(count)])


def gather_weight(mine, other, y_hi):
    crossed = flip(other, Y, 3, 4)
    first = jnp.where(y_hi == 0, jnp.stack([mine, crossed]), jnp.stack([crossed, mine]))
    own, rest = {0: first}, {}

    def hand_over(keys):
        low = flip(jnp.stack([own[k][0] for k in keys]), Y, 2, 4)
        high = flip(jnp.stack([own[k][1] for k in keys]), Y, 3, 4)
        for i, k in enumerate(keys):
            rest[k] = ((low, i), (high, i))

    right = left = first
    for step in range(1, 4):
        right = shift(right, "z", 1, NZ)
        left = shift(left, "z", NZ - 1, NZ)
        own[NZ - step], own[step] = right, left
        hand_over([0, NZ - 1, 1] if step == 1 else [NZ - step, step])
    far_low = shift(right[0:1], "z", 1, NZ)
    far_high = shift(left[1:2], "z", NZ - 1, NZ)
    far = ((far_low, 0), (far_high, 0))
    rest[4] = ((flip(far_low, Y, 2, 4), 0), (flip(far_high, Y, 3, 4), 0))
    own = [far if k == 4 else ((own[k], 0), (own[k], 1)) for k in range(NZ)]
    return own, [rest[k] for k in range(NZ)]


def forward_kernel(places, count, normed, *refs):
    weights = refs[:count]
    attended, probs, partial, out_w, qkv_w, qkv = refs[count:]
    image, tile = pl.program_id(0), pl.program_id(1)
    tile_rows = normed.shape[1]

    @pl.when((image == 0) & (tile == 0))
    def _():
        for e in range(2):
            for k in range(2 * NZ):
                which, index = places[e][k]
                block = weights[which][index]
                rows = slice(k * 192, k * 192 + 192)
                qkv_w[rows, e * 384 : e * 384 + 384] = block[:, :384]
                out_w[rows, e * HD : e * HD + HD] = block[:, 384:]

    product = jnp.dot(normed[0], qkv_w[...], preferred_element_type=f32)
    start = pl.multiple_of(tile * tile_rows, tile_rows)
    qkv[pl.ds(start, tile_rows), :] = product.astype(bf16)

    @pl.when(tile == pl.num_programs(1) - 1)
    def _():
        for e in range(2):
            base = e * 384
            query, keys = qkv[:, base : base + HD], qkv[:, base + HD : base + 2 * HD]
            scores = lax.dot_general(
                query, keys, (((1,), (1,)), ((), ())), preferred_element_type=f32
            ) * (1.0 / math.sqrt(HD))
            weight = jnp.exp(scores - jnp.max(scores, axis=-1, keepdims=True))
            prob = (weight / jnp.sum(weight, axis=-1, keepdims=True)).astype(bf16)
            probs[0, e] = prob
            attended[0, :, e * HD : e * HD + HD] = jnp.dot(
                prob, qkv[:, base + 2 * HD : base + 384], preferred_element_type=f32
            ).astype(bf16)
        for chunk in range(4):
            part = slice(chunk * 768, chunk * 768 + 768)
            partial[0, :, part] = lax.dot_general(
                attended[0], out_w[part, :], (((1,), (1,)), ((), ())), preferred_element_type=f32
            ).astype(bf16)


def forward(normed, own, rest):
    arrays, places = [], []
    for blocks in (own, rest):
        places.append([])
        for pair in blocks:
            for array, index in pair:
                known = [i for i, a in enumerate(arrays) if a is array]
                if not known:
                    arrays.append(array)
                    known = [len(arrays) - 1]
                places[-1].append((known[0], index))
    _, length, width = normed.shape
    tiles = 2
    shapes = (
        ((2, length, 2 * HD), (1, length, 2 * HD), lambda i, t: (i, 0, 0)),
        ((2, 2, length, length), (1, 2, length, length), lambda i, t: (i, 0, 0, 0)),
        ((2, length, width), (1, length, width), lambda i, t: (i, 0, 0)),
        ((width, 2 * HD), (width, 2 * HD), lambda i, t: (0, 0)),
    )
    return pl.pallas_call(
        functools.partial(forward_kernel, places, len(arrays)),
        grid=(2, tiles),
        in_specs=[pl.BlockSpec((1, length // tiles, width), lambda i, t: (i, t, 0))]
        + [pl.BlockSpec(a.shape, lambda i, t: (0, 0, 0)) for a in arrays],
        out_specs=[pl.BlockSpec(block, index) for _, block, index in shapes],
        out_shape=[jax.ShapeDtypeStruct(shape, bf16) for shape, _, _ in shapes],
        scratch_shapes=[
            pltpu.VMEM((width, 6 * HD), bf16),
            pltpu.VMEM((length, 6 * HD), bf16),
        ],
        compiler_params=pltpu.CompilerParams(vmem_limit_bytes=60 * 2**20),
        name="forward",
    )(normed, *arrays)


def store_placed(grad, position, total):
    z, dp = position[0], position[1]
    for k in range(NZ):
        block = total[:, k * 384 : k * 384 + 384].astype(bf16)
        start = pl.multiple_of(lax.rem(z + k, NZ) * 384, 384)
        for e in range(2):
            column = pl.multiple_of((dp ^ e) * HD, HD)
            grad[pl.ds(start, 384), pl.ds(column, HD)] = block[e * HD : e * HD + HD].T


def grad_out_kernel(position, scale, residual, attended, grad, total):
    image = pl.program_id(0)
    term = jnp.dot(attended[0].T, residual[0], preferred_element_type=f32) * scale[image]

    @pl.when(image == 0)
    def _():
        total[...] = term

    @pl.when(image == 1)
    def _():
        total[...] += term
        store_placed(grad, position, total)


def grad_value_kernel(position, scale, residual, normed, probs, out_w, grad, total):
    image = pl.program_id(0)
    d_attended = jnp.dot(residual[0], out_w[...], preferred_element_type=f32) * scale[image]
    d_attended = d_attended.astype(bf16)
    d_values = jnp.concatenate(
        [
            lax.dot_general(
                d_attended[:, e * HD : e * HD + HD].T, probs[0, e], (((1,), (0,)), ((), ())),
                preferred_element_type=f32,
            ).astype(bf16)
            for e in range(2)
        ],
        axis=0,
    )
    term = jnp.dot(d_values, normed[0], preferred_element_type=f32)

    @pl.when(image == 0)
    def _():
        total[...] = term

    @pl.when(image == 1)
    def _():
        total[...] += term
        store_placed(grad, position, total)


def gradient(kernel, name, position, scale, images, shared):
    width = images[0].shape[2]

    def image_spec(a):
        zeros = (0,) * (a.ndim - 1)
        return pl.BlockSpec((1,) + a.shape[1:], lambda i: (i,) + zeros)

    smem = pl.BlockSpec(memory_space=pltpu.SMEM)
    return pl.pallas_call(
        kernel,
        grid=(2,),
        in_specs=[smem, smem]
        + [image_spec(a) for a in images]
        + [pl.BlockSpec(a.shape, lambda i: (0, 0)) for a in shared],
        out_specs=pl.BlockSpec((width, 2 * HD), lambda i: (0, 0)),
        out_shape=jax.ShapeDtypeStruct((width, 2 * HD), bf16),
        scratch_shapes=[pltpu.VMEM((2 * HD, width), f32)],
        compiler_params=pltpu.CompilerParams(vmem_limit_bytes=60 * 2**20),
        name=name,
    )(position, scale, *images, *shared)


def reduce_y(grad, dp, y_hi):
    pieces = grad.reshape(2, NZ, 2, -1, grad.shape[1])

    def piece(mask, part):
        chosen = lax.dynamic_index_in_dim(pieces, dp ^ (mask >> 1), 0, keepdims=False)
        chosen = lax.dynamic_index_in_dim(chosen, y_hi ^ (mask & 1), 1, keepdims=False)
        return chosen[part]

    sums = []
    for part, near, across in ((slice(0, 4), 2, 3), (slice(4, 8), 3, 2)):
        came = flip(jnp.stack([piece(near, part), piece(1, part)]), Y, near, 4).astype(f32)
        passed = (piece(across, part).astype(f32) + came[1]).astype(bf16)
        sums.append(piece(0, part).astype(f32) + came[0] + flip(passed, Y, across, 4).astype(f32))
    return jnp.concatenate(sums, axis=0).astype(bf16)


def reduce_z(shares, z):
    result = None
    for step in range(NZ):
        piece = lax.dynamic_index_in_dim(shares, (z + step) % NZ, 1, keepdims=False)
        term = (piece if step == 0 else shift(piece, "z", step, NZ)).astype(f32)
        result = term if result is None else result + term
    return result.astype(bf16)


def body(latents, noise, timesteps, ref_errors, norm_gain, w_query, w_key, w_value, w_out):
    dp, z, y_hi = lax.axis_index("dp"), lax.axis_index("z"), lax.axis_index("yh")
    local_len, model_width = latents.shape[1], latents.shape[3]
    full_len = local_len * 8
    z_rows = model_width // NZ

    def rolled(value, offset, axis):
        twice = jnp.concatenate([value, value], axis=axis)
        return lax.dynamic_slice_in_dim(twice, offset * z_rows, model_width, axis)

    def head(weight, which):
        return jnp.where(which == 0, weight[:, :HD], weight[:, HD:])

    def heads(which):
        return jnp.concatenate([head(w, which) for w in (w_query, w_key, w_value, w_out.T)], axis=1)

    own, rest = gather_weight(heads(dp), heads(1 - dp), y_hi)

    clean32 = rolled(latents[0], z, 2).transpose(1, 0, 2).astype(f32)
    noise32 = rolled(noise[0], z, 2).transpose(1, 0, 2).astype(f32)
    gain = rolled(norm_gain, z, 0)
    sigma = (timesteps[0].astype(f32) + 0.5) / NSTEP
    mixing = sigma[:, None, None]
    noised = ((1.0 - mixing) * clean32 + mixing * noise32).astype(bf16).astype(f32)
    target = noise32 - clean32
    inverse = lax.rsqrt(jnp.mean(noised * noised, axis=-1, keepdims=True) + norm_epsilon)
    normed = (noised * inverse * gain).astype(bf16)
    normed = lax.all_gather(normed, SEQ, axis=1, tiled=True)
    attended, probs, partial, out_w = forward(normed, own, rest)
    predicted = lax.psum_scatter(
        partial, SEQ, scatter_dimension=1, tiled=True
    ).astype(f32)
    differ = predicted - target
    residual = lax.all_gather(differ.astype(bf16), SEQ, axis=1, tiled=True)
    sums = jnp.sum(differ * differ, axis=(1, 2))
    sums = sums + flip(sums, "core", 1, 2)
    sums = sums + flip(sums, "x", 1, 4)
    sums = sums + flip(sums, "x", 2, 4)
    errors = sums / (full_len * model_width)
    reference_pair = ref_errors[0]
    margin = errors[0] - reference_pair[0] - (errors[1] - reference_pair[1])
    pair_loss = jax.nn.softplus(preference_beta * margin)
    weight_pair = (
        preference_beta
        * jax.nn.sigmoid(preference_beta * margin)
        * 2.0
        * LOSS_SCALE
        / (full_len * model_width)
    )
    image_scale = jnp.array([1.0, -1.0], f32) * weight_pair

    position = jnp.stack([z, dp]).astype(jnp.int32)
    grad_out = gradient(
        grad_out_kernel, "grad_out", position, image_scale, (residual, attended), ()
    )
    out_share = reduce_y(grad_out, dp, y_hi)
    grad_value = gradient(
        grad_value_kernel, "grad_value", position, image_scale, (residual, normed, probs), (out_w,)
    )
    value_share = reduce_y(grad_value, dp, y_hi)
    summed = reduce_z(jnp.stack([value_share, out_share]), z)
    return summed[0], summed[1].T, pair_loss.reshape(1)


def solution(mesh):
    fine = Mesh(mesh.devices.reshape(2, NZ, 2, 4, 2), ("dp", "z", "yh", "x", "core"))
    fsdp = ("z", "yh")
    in_specs = (
        P(GROUP, SEQ, None, None),
        P(GROUP, SEQ, None, None),
        P(GROUP, None),
        P(GROUP, None),
        P(),
        P(fsdp, SEQ),
        P(fsdp, SEQ),
        P(fsdp, SEQ),
        P(SEQ, fsdp),
    )
    out_specs = (P(GROUP, SEQ), P(SEQ, GROUP), P(GROUP))
    return jax.shard_map(body, mesh=fine, in_specs=in_specs, out_specs=out_specs, check_vma=False)
```

```python
import functools
import math

import jax
import jax.numpy as jnp
from jax import lax
from jax.experimental import pallas as pl
from jax.experimental.pallas import tpu as pltpu
from jax.sharding import Mesh, PartitionSpec as P

HD = 128
NSTEP = 1000
LOSS_SCALE = 24576
NZ = 8

preference_beta = 2.0
norm_epsilon = 1e-06

SEQ = ("x", "core")
GROUP = ("dp", "z", "yh")
Y = ("dp", "yh")
bf16 = jnp.bfloat16
f32 = jnp.float32


def shift(value, axis, step, count):
    return lax.ppermute(value, axis, [(i, (i + step) % count) for i in range(count)])


def flip(value, axis, mask, count):
    return lax.ppermute(value, axis, [(i, i ^ mask) for i in range(count)])


def gather_weight(mine, crossed, y_hi):
    first = jnp.where(y_hi == 0, jnp.stack([mine, crossed]), jnp.stack([crossed, mine]))
    own, rest = {0: first}, {}

    def hand_over(keys):
        low = flip(jnp.stack([own[k][0] for k in keys]), Y, 2, 4)
        high = flip(jnp.stack([own[k][1] for k in keys]), Y, 3, 4)
        for i, k in enumerate(keys):
            rest[k] = ((low, i), (high, i))

    right = left = first
    for step in range(1, 4):
        right = shift(right, "z", 1, NZ)
        left = shift(left, "z", NZ - 1, NZ)
        own[NZ - step], own[step] = right, left
        hand_over([0, NZ - 1, 1] if step == 1 else [NZ - step, step])
    far_low = shift(right[0:1], "z", 1, NZ)
    far_high = shift(left[1:2], "z", NZ - 1, NZ)
    far = ((far_low, 0), (far_high, 0))
    rest[4] = ((flip(far_low, Y, 2, 4), 0), (flip(far_high, Y, 3, 4), 0))
    own = [far if k == 4 else ((own[k], 0), (own[k], 1)) for k in range(NZ)]
    return own, [rest[k] for k in range(NZ)]


def forward_kernel(places, count, position, normed, *refs):
    weights = refs[:count]
    attended, probs, partial, out_w, qkv_w, qkv = refs[count:]
    image, tile = pl.program_id(0), pl.program_id(1)
    tile_rows = normed.shape[1]

    @pl.when((image == 0) & (tile == 0))
    def _():
        for e in range(2):
            for k in range(2 * NZ):
                which, index = places[e][k]
                block = weights[which][index]
                start = lax.rem(position[0] + k // 2, NZ) * 384 + (k % 2) * 192
                rows = pl.ds(pl.multiple_of(start, 192), 192)
                qkv_w[rows, e * 384 : e * 384 + 384] = block[:, :384]
                out_w[rows, e * HD : e * HD + HD] = block[:, 384:]

    product = jnp.dot(normed[0], qkv_w[...], preferred_element_type=f32)
    start = pl.multiple_of(tile * tile_rows, tile_rows)
    qkv[pl.ds(start, tile_rows), :] = product.astype(bf16)

    @pl.when(tile == pl.num_programs(1) - 1)
    def _():
        for e in range(2):
            base = e * 384
            query, keys = qkv[:, base : base + HD], qkv[:, base + HD : base + 2 * HD]
            scores = lax.dot_general(
                query, keys, (((1,), (1,)), ((), ())), preferred_element_type=f32
            ) * (1.0 / math.sqrt(HD))
            weight = jnp.exp(scores - jnp.max(scores, axis=-1, keepdims=True))
            prob = (weight / jnp.sum(weight, axis=-1, keepdims=True)).astype(bf16)
            probs[0, e] = prob
            attended[0, :, e * HD : e * HD + HD] = jnp.dot(
                prob, qkv[:, base + 2 * HD : base + 384], preferred_element_type=f32
            ).astype(bf16)
        for chunk in range(4):
            part = slice(chunk * 768, chunk * 768 + 768)
            partial[0, :, part] = lax.dot_general(
                attended[0], out_w[part, :], (((1,), (1,)), ((), ())), preferred_element_type=f32
            ).astype(bf16)


def forward(position, normed, own, rest):
    arrays, places = [], []
    for blocks in (own, rest):
        places.append([])
        for pair in blocks:
            for array, index in pair:
                known = [i for i, a in enumerate(arrays) if a is array]
                if not known:
                    arrays.append(array)
                    known = [len(arrays) - 1]
                places[-1].append((known[0], index))
    _, length, width = normed.shape
    tiles = 2
    shapes = (
        ((2, length, 2 * HD), (1, length, 2 * HD), lambda i, t: (i, 0, 0)),
        ((2, 2, length, length), (1, 2, length, length), lambda i, t: (i, 0, 0, 0)),
        ((2, length, width), (1, length, width), lambda i, t: (i, 0, 0)),
        ((width, 2 * HD), (width, 2 * HD), lambda i, t: (0, 0)),
    )
    return pl.pallas_call(
        functools.partial(forward_kernel, places, len(arrays)),
        grid=(2, tiles),
        in_specs=[
            pl.BlockSpec(memory_space=pltpu.SMEM),
            pl.BlockSpec((1, length // tiles, width), lambda i, t: (i, t, 0)),
        ]
        + [pl.BlockSpec(a.shape, lambda i, t: (0, 0, 0)) for a in arrays],
        out_specs=[pl.BlockSpec(block, index) for _, block, index in shapes],
        out_shape=[jax.ShapeDtypeStruct(shape, bf16) for shape, _, _ in shapes],
        scratch_shapes=[
            pltpu.VMEM((width, 6 * HD), bf16),
            pltpu.VMEM((length, 6 * HD), bf16),
        ],
        compiler_params=pltpu.CompilerParams(vmem_limit_bytes=60 * 2**20),
        cost_estimate=pl.CostEstimate(flops=14_000_000_000, bytes_accessed=14_000_000, transcendentals=0),
        name="forward",
    )(position, normed, *arrays)


def store_heads(grad, index, rows, position, block):
    block = block.astype(bf16)
    for e in range(2):
        column = pl.multiple_of((position[1] ^ e) * HD, HD)
        grad[index + (rows, pl.ds(column, HD))] = block[e * HD : e * HD + HD].T


def gather_tokens(own):
    left = shift(own, "x", 1, 4)
    right = shift(own, "x", 3, 4)
    far_0 = shift(left[0:1], "x", 1, 4)
    far_1 = shift(right[1:2], "x", 3, 4)
    found = []
    for array, image, offset in (
        (own, None, 0), (left, None, 3), (right, None, 1), (far_0, 0, 2), (far_1, 1, 2)
    ):
        found.append((array, image, offset, 0))
        found.append((flip(array, "core", 1, 2), image, offset, 1))
    return found


def chunk_kernel(places, chunk, position, scale, attended, out_w, *refs):
    blocks = refs[: len(places)]
    grad, part, held, total = refs[len(places) :]
    tokens = blocks[0].shape[1]
    for block, (image, offset, swap) in zip(blocks, places):
        spot = lax.rem(position[2] + offset, 4) * 2 + (position[3] ^ swap)
        rows = pl.ds(pl.multiple_of(spot * tokens, tokens), tokens)
        for i in range(2) if image is None else (image,):
            held[i, rows, :] = block[i if image is None else 0]
    half = held.shape[2] // 2
    for i in range(2):
        product = None
        for owner in range(2):
            term = jnp.dot(
                held[i, :, owner * half : owner * half + half],
                out_w[owner, chunk],
                preferred_element_type=f32,
            )
            product = term if product is None else product + term
        part[i] = product
        term = jnp.dot(attended[i].T, held[i], preferred_element_type=f32) * scale[i]
        if i == 0:
            total[...] = term
        else:
            total[...] += term
    for k in range(4):
        rows = slice((k % 2) * 384, (k % 2) * 384 + 384)
        store_heads(grad, (k // 2,), rows, position, total[:, k * 384 : k * 384 + 384])


def chunk_gradient(chunk, position, scale, attended, out_w, found):
    arrays = [entry[0] for entry in found]
    width = arrays[0].shape[2]
    length = attended.shape[1]
    smem = pl.BlockSpec(memory_space=pltpu.SMEM)
    vmem = pl.BlockSpec(memory_space=pltpu.VMEM)
    return pl.pallas_call(
        functools.partial(chunk_kernel, [entry[1:] for entry in found], chunk),
        in_specs=[smem, smem] + [vmem] * (2 + len(arrays)),
        out_specs=[vmem, vmem],
        out_shape=[
            jax.ShapeDtypeStruct((2, width // 2, 2 * HD), bf16),
            jax.ShapeDtypeStruct((2, length, 2 * HD), f32),
        ],
        scratch_shapes=[pltpu.VMEM((2, length, width), bf16), pltpu.VMEM((2 * HD, width), f32)],
        compiler_params=pltpu.CompilerParams(vmem_limit_bytes=60 * 2**20),
        cost_estimate=pl.CostEstimate(flops=7_000_000_000, bytes_accessed=7_000_000, transcendentals=0),
        name="chunk_gradient",
    )(position, scale, attended, out_w.reshape(2, 2, width // 2, 2 * HD), *arrays)


def grad_value_kernel(position, scale, part_0, part_1, normed, probs, grad, total):
    image = pl.program_id(0)
    d_attended = ((part_0[0] + part_1[0]) * scale[image]).astype(bf16)
    d_values = jnp.concatenate(
        [
            lax.dot_general(
                d_attended[:, e * HD : e * HD + HD].T, probs[0, e], (((1,), (0,)), ((), ())),
                preferred_element_type=f32,
            ).astype(bf16)
            for e in range(2)
        ],
        axis=0,
    )
    term = jnp.dot(d_values, normed[0], preferred_element_type=f32)

    @pl.when(image == 0)
    def _():
        total[...] = term

    @pl.when(image == 1)
    def _():
        total[...] += term
        for k in range(NZ):
            part = slice(k * 384, k * 384 + 384)
            store_heads(grad, (), part, position, total[:, part])


def value_gradient(position, scale, *images):
    width = images[2].shape[2]

    def image_spec(a):
        zeros = (0,) * (a.ndim - 1)
        return pl.BlockSpec((1,) + a.shape[1:], lambda i: (i,) + zeros)

    smem = pl.BlockSpec(memory_space=pltpu.SMEM)
    return pl.pallas_call(
        grad_value_kernel,
        grid=(2,),
        in_specs=[smem, smem] + [image_spec(a) for a in images],
        out_specs=pl.BlockSpec((width, 2 * HD), lambda i: (0, 0)),
        out_shape=jax.ShapeDtypeStruct((width, 2 * HD), bf16),
        scratch_shapes=[pltpu.VMEM((2 * HD, width), f32)],
        compiler_params=pltpu.CompilerParams(vmem_limit_bytes=60 * 2**20),
        cost_estimate=pl.CostEstimate(flops=10_000_000_000, bytes_accessed=10_000_000, transcendentals=0),
        name="grad_value",
    )(position, scale, *images)


def start_y(pieces, dp, y_hi, near):
    def piece(mask):
        chosen = lax.dynamic_index_in_dim(pieces, dp ^ (mask >> 1), 0, keepdims=False)
        return lax.dynamic_index_in_dim(chosen, y_hi ^ (mask & 1), 1, keepdims=False)

    return jnp.stack([piece(near), piece(1)]), piece(5 - near), piece(0)


def finish_y(came, kept, near):
    came = came.astype(f32)
    passed = (kept[0].astype(f32) + came[1]).astype(bf16)
    passed = flip(passed, Y, 5 - near, 4).astype(f32)
    return (kept[1].astype(f32) + came[0] + passed).astype(bf16)


def reduce_z(shares, z):
    result = None
    for step in range(NZ):
        piece = lax.dynamic_index_in_dim(shares, (z + step) % NZ, 1, keepdims=False)
        term = (piece if step == 0 else shift(piece, "z", step, NZ)).astype(f32)
        result = term if result is None else result + term
    return result.astype(bf16)


def body(latents, noise, timesteps, ref_errors, norm_gain, w_query, w_key, w_value, w_out):
    dp, z, y_hi = lax.axis_index("dp"), lax.axis_index("z"), lax.axis_index("yh")
    local_len, model_width = latents.shape[1], latents.shape[3]
    full_len = local_len * 8

    def head(weight, which):
        return jnp.where(which == 0, weight[:, :HD], weight[:, HD:])

    def heads(which):
        return jnp.concatenate([head(w, which) for w in (w_query, w_key, w_value, w_out.T)], axis=1)

    position = [z, dp, lax.axis_index("x"), lax.axis_index("core")]
    position = jnp.stack(position).astype(jnp.int32)
    crossed = flip(heads(1 - dp), Y, 3, 4)

    clean32 = latents[0].transpose(1, 0, 2).astype(f32)
    noise32 = noise[0].transpose(1, 0, 2).astype(f32)
    sigma = (timesteps[0].astype(f32) + 0.5) / NSTEP
    mixing = sigma[:, None, None]
    noised = ((1.0 - mixing) * clean32 + mixing * noise32).astype(bf16).astype(f32)
    target = noise32 - clean32
    inverse = lax.rsqrt(jnp.mean(noised * noised, axis=-1, keepdims=True) + norm_epsilon)
    normed = (noised * inverse * norm_gain).astype(bf16)
    normed, crossed = lax.optimization_barrier((normed, crossed))
    own, rest = gather_weight(heads(dp), crossed, y_hi)
    normed = lax.all_gather(normed, SEQ, axis=1, tiled=True)
    attended, probs, partial, out_w = forward(position, normed, own, rest)
    predicted = lax.psum_scatter(
        partial, SEQ, scatter_dimension=1, tiled=True
    ).astype(f32)
    differ = predicted - target
    residual = differ.astype(bf16).reshape(2, local_len, 2, 2, model_width // 4)
    found = [
        gather_tokens(residual[:, :, :, chunk].reshape(2, local_len, model_width // 2))
        for chunk in range(2)
    ]
    sums = jnp.sum(differ * differ, axis=(1, 2))
    sums = sums + flip(sums, "core", 1, 2)
    sums = sums + flip(sums, "x", 1, 4)
    sums = sums + flip(sums, "x", 2, 4)
    errors = sums / (full_len * model_width)
    reference_pair = ref_errors[0]
    margin = errors[0] - reference_pair[0] - (errors[1] - reference_pair[1])
    pair_loss = jax.nn.softplus(preference_beta * margin)
    weight_pair = (
        preference_beta
        * jax.nn.sigmoid(preference_beta * margin)
        * 2.0
        * LOSS_SCALE
        / (full_len * model_width)
    )
    image_scale = jnp.array([1.0, -1.0], f32) * weight_pair

    def first(chunk, scale):
        grad, part = chunk_gradient(chunk, position, scale, attended, out_w, found[chunk])
        send, *kept = start_y(grad.reshape(2, 4, 2, -1, 2 * HD), dp, y_hi, 2 + chunk)
        return part, send, kept

    part_0, send_0, kept_0 = first(0, image_scale)
    came_0, scale_1 = lax.optimization_barrier((flip(send_0, Y, 2, 4), image_scale))
    part_1, send_1, kept_1 = first(1, scale_1)
    out_share_0 = finish_y(came_0, kept_0, 2)
    out_share_0, send_1, scale_2 = lax.optimization_barrier((out_share_0, send_1, scale_1))
    came_1 = flip(send_1, Y, 3, 4)
    grad_value = value_gradient(position, scale_2, part_0, part_1, normed, probs)
    grad_value, came_1 = lax.optimization_barrier((grad_value, came_1))
    pieces = grad_value.reshape(2, NZ, 2, -1, 2 * HD)
    value_shares = []
    for half in range(2):
        send, *kept = start_y(pieces[:, 4 * half : 4 * half + 4], dp, y_hi, 2 + half)
        value_shares.append(finish_y(flip(send, Y, 2 + half, 4), kept, 2 + half))
    out_shares = [out_share_0, finish_y(came_1, kept_1, 3)]
    shares = jnp.stack([jnp.concatenate(value_shares), jnp.concatenate(out_shares)])
    summed = reduce_z(shares, z)
    return summed[0], summed[1].T, pair_loss.reshape(1)


def solution(mesh):
    fine = Mesh(mesh.devices.reshape(2, NZ, 2, 4, 2), ("dp", "z", "yh", "x", "core"))
    fsdp = ("z", "yh")
    in_specs = (
        P(GROUP, SEQ, None, None),
        P(GROUP, SEQ, None, None),
        P(GROUP, None),
        P(GROUP, None),
        P(),
        P(fsdp, SEQ),
        P(fsdp, SEQ),
        P(fsdp, SEQ),
        P(SEQ, fsdp),
    )
    out_specs = (P(GROUP, SEQ), P(SEQ, GROUP), P(GROUP))
    return jax.shard_map(body, mesh=fine, in_specs=in_specs, out_specs=out_specs, check_vma=False)
```

```python
import functools
import math

import jax
import jax.numpy as jnp
from jax import lax
from jax.experimental import pallas as pl
from jax.experimental.pallas import tpu as pltpu
from jax.sharding import Mesh, PartitionSpec as P

HD = 128
NSTEP = 1000
LOSS_SCALE = 24576
NZ = 8

preference_beta = 2.0
norm_epsilon = 1e-06

SEQ = ("x", "core")
GROUP = ("dp", "z", "yh")
Y = ("dp", "yh")
bf16 = jnp.bfloat16
f32 = jnp.float32


def shift(value, axis, step, count):
    return lax.ppermute(value, axis, [(i, (i + step) % count) for i in range(count)])


def flip(value, axis, mask, count):
    return lax.ppermute(value, axis, [(i, i ^ mask) for i in range(count)])


def gather_weight(mine, crossed, y_hi):
    first = jnp.where(y_hi == 0, jnp.stack([mine, crossed]), jnp.stack([crossed, mine]))
    own, rest = {0: first}, {}

    def hand_over(keys):
        low = flip(jnp.stack([own[k][0] for k in keys]), Y, 2, 4)
        high = flip(jnp.stack([own[k][1] for k in keys]), Y, 3, 4)
        for i, k in enumerate(keys):
            rest[k] = ((low, i), (high, i))

    right = left = first
    for step in range(1, 4):
        right = shift(right, "z", 1, NZ)
        left = shift(left, "z", NZ - 1, NZ)
        own[NZ - step], own[step] = right, left
        hand_over([0, NZ - 1, 1] if step == 1 else [NZ - step, step])
    far_low = shift(right[0:1], "z", 1, NZ)
    far_high = shift(left[1:2], "z", NZ - 1, NZ)
    far = ((far_low, 0), (far_high, 0))
    rest[4] = ((flip(far_low, Y, 2, 4), 0), (flip(far_high, Y, 3, 4), 0))
    own = [far if k == 4 else ((own[k], 0), (own[k], 1)) for k in range(NZ)]
    return own, [rest[k] for k in range(NZ)]


def forward_kernel(places, count, position, normed, *refs):
    weights = refs[:count]
    attended, probs, partial, blocks, out_w, qkv_w, qkv = refs[count:]
    image, tile = pl.program_id(0), pl.program_id(1)
    tile_rows = normed.shape[1]

    @pl.when((image == 0) & (tile == 0))
    def _():
        for e in range(2):
            for k in range(2 * NZ):
                which, index = places[e][k]
                block = weights[which][index]
                start = lax.rem(position[0] + k // 2, NZ) * 384 + (k % 2) * 192
                rows = pl.ds(pl.multiple_of(start, 192), 192)
                qkv_w[rows, e * 384 : e * 384 + 384] = block[:, :384]
                out_w[rows, e * HD : e * HD + HD] = block[:, 384:]

    product = jnp.dot(normed[0], qkv_w[...], preferred_element_type=f32)
    start = pl.multiple_of(tile * tile_rows, tile_rows)
    qkv[pl.ds(start, tile_rows), :] = product.astype(bf16)

    @pl.when(tile == pl.num_programs(1) - 1)
    def _():
        for e in range(2):
            base = e * 384
            query, keys = qkv[:, base : base + HD], qkv[:, base + HD : base + 2 * HD]
            scores = lax.dot_general(
                query, keys, (((1,), (1,)), ((), ())), preferred_element_type=f32
            ) * (1.0 / math.sqrt(HD))
            weight = jnp.exp(scores - jnp.max(scores, axis=-1, keepdims=True))
            prob = (weight / jnp.sum(weight, axis=-1, keepdims=True)).astype(bf16)
            probs[0, e] = prob
            attended[0, :, e * HD : e * HD + HD] = jnp.dot(
                prob, qkv[:, base + 2 * HD : base + 384], preferred_element_type=f32
            ).astype(bf16)
        tokens = blocks.shape[3]
        for part in range(4):
            owner, chunk = part // 2, part % 2
            columns = slice(owner * 768, owner * 768 + 768)
            product = lax.dot_general(
                attended[0],
                out_w[part * 768 : part * 768 + 768, :],
                (((1,), (1,)), ((), ())),
                preferred_element_type=f32,
            ).astype(bf16)
            if chunk == 1:
                partial[0, :, columns] = product
                continue
            for spot in range(8):
                swap = (spot % 2) ^ position[3]
                offset = lax.rem(spot // 2 + 4 - position[2], 4)
                rows = slice(spot * tokens, spot * tokens + tokens)
                blocks[swap, offset, 0, :, columns] = product[rows]


def forward(position, normed, own, rest):
    arrays, places = [], []
    for blocks in (own, rest):
        places.append([])
        for pair in blocks:
            for array, index in pair:
                known = [i for i, a in enumerate(arrays) if a is array]
                if not known:
                    arrays.append(array)
                    known = [len(arrays) - 1]
                places[-1].append((known[0], index))
    _, length, width = normed.shape
    tiles = 2
    shapes = (
        ((2, length, 2 * HD), (1, length, 2 * HD), lambda i, t: (i, 0, 0)),
        ((2, 2, length, length), (1, 2, length, length), lambda i, t: (i, 0, 0, 0)),
        ((2, length, width // 2), (1, length, width // 2), lambda i, t: (i, 0, 0)),
        (
            (2, 4, 2, length // 8, width // 2),
            (2, 4, 1, length // 8, width // 2),
            lambda i, t: (0, 0, i, 0, 0),
        ),
        ((width, 2 * HD), (width, 2 * HD), lambda i, t: (0, 0)),
    )
    return pl.pallas_call(
        functools.partial(forward_kernel, places, len(arrays)),
        grid=(2, tiles),
        in_specs=[
            pl.BlockSpec(memory_space=pltpu.SMEM),
            pl.BlockSpec((1, length // tiles, width), lambda i, t: (i, t, 0)),
        ]
        + [pl.BlockSpec(a.shape, lambda i, t: (0, 0, 0)) for a in arrays],
        out_specs=[pl.BlockSpec(block, index) for _, block, index in shapes],
        out_shape=[jax.ShapeDtypeStruct(shape, bf16) for shape, _, _ in shapes],
        scratch_shapes=[
            pltpu.VMEM((width, 6 * HD), bf16),
            pltpu.VMEM((length, 6 * HD), bf16),
        ],
        compiler_params=pltpu.CompilerParams(vmem_limit_bytes=60 * 2**20),
        cost_estimate=pl.CostEstimate(flops=14_000_000_000, bytes_accessed=14_000_000, transcendentals=0),
        name="forward",
    )(position, normed, *arrays)


def store_heads(grad, index, rows, position, block):
    block = block.astype(bf16)
    for e in range(2):
        column = pl.multiple_of((position[1] ^ e) * HD, HD)
        grad[index + (rows, pl.ds(column, HD))] = block[e * HD : e * HD + HD].T


def sum_tokens(blocks):
    crossed = flip(blocks[1], "core", 1, 2)
    pair = (blocks[0].astype(f32) + crossed.astype(f32)).astype(bf16)
    total = pair[0].astype(f32)
    for offset in (1, 3, 2):
        total = total + shift(pair[offset], "x", offset, 4).astype(f32)
    return total


def gather_tokens(own):
    found = []
    for offset in (0, 3, 1, 2):
        array = own if offset == 0 else shift(own, "x", 4 - offset, 4)
        found.append((array, offset, 0))
        found.append((flip(array, "core", 1, 2), offset, 1))
    return found


def chunk_kernel(places, chunk, position, scale, attended, out_w, *refs):
    blocks = refs[: len(places)]
    grad, part, total = refs[len(places) : len(places) + 3]
    held = blocks[0] if places[0] is None else refs[-1]
    if places[0] is not None:
        tokens = blocks[0].shape[1]
        for block, (offset, swap) in zip(blocks, places):
            spot = lax.rem(position[2] + offset, 4) * 2 + (position[3] ^ swap)
            rows = pl.ds(pl.multiple_of(spot * tokens, tokens), tokens)
            for i in range(2):
                held[i, rows, :] = block[i]
    half = held.shape[2] // 2
    for i in range(2):
        product = None
        for owner in range(2):
            term = jnp.dot(
                held[i, :, owner * half : owner * half + half],
                out_w[owner, chunk],
                preferred_element_type=f32,
            )
            product = term if product is None else product + term
        part[i] = product
        term = jnp.dot(attended[i].T, held[i], preferred_element_type=f32) * scale[i]
        if i == 0:
            total[...] = term
        else:
            total[...] += term
    for k in range(4):
        rows = slice((k % 2) * 384, (k % 2) * 384 + 384)
        store_heads(grad, (k // 2,), rows, position, total[:, k * 384 : k * 384 + 384])


def chunk_gradient(chunk, position, scale, attended, out_w, found):
    arrays = [entry[0] for entry in found]
    places = [entry[1:] or None for entry in found]
    width = arrays[0].shape[2]
    length = attended.shape[1]
    smem = pl.BlockSpec(memory_space=pltpu.SMEM)
    vmem = pl.BlockSpec(memory_space=pltpu.VMEM)
    held = [pltpu.VMEM((2, length, width), bf16)] if places[0] else []
    return pl.pallas_call(
        functools.partial(chunk_kernel, places, chunk),
        in_specs=[smem, smem] + [vmem] * (2 + len(arrays)),
        out_specs=[vmem, vmem],
        out_shape=[
            jax.ShapeDtypeStruct((2, width // 2, 2 * HD), bf16),
            jax.ShapeDtypeStruct((2, length, 2 * HD), f32),
        ],
        scratch_shapes=[pltpu.VMEM((2 * HD, width), f32)] + held,
        compiler_params=pltpu.CompilerParams(vmem_limit_bytes=60 * 2**20),
        cost_estimate=pl.CostEstimate(
            flops=7_000_000_000, bytes_accessed=7_000_000, transcendentals=0
        ),
        name="chunk_gradient",
    )(position, scale, attended, out_w.reshape(2, 2, width // 2, 2 * HD), *arrays)


def grad_value_kernel(position, scale, part_0, part_1, normed, probs, grad, total):
    image = pl.program_id(0)
    d_attended = ((part_0[0] + part_1[0]) * scale[image]).astype(bf16)
    d_values = jnp.concatenate(
        [
            lax.dot_general(
                d_attended[:, e * HD : e * HD + HD].T, probs[0, e], (((1,), (0,)), ((), ())),
                preferred_element_type=f32,
            ).astype(bf16)
            for e in range(2)
        ],
        axis=0,
    )
    term = jnp.dot(d_values, normed[0], preferred_element_type=f32)

    @pl.when(image == 0)
    def _():
        total[...] = term

    @pl.when(image == 1)
    def _():
        total[...] += term
        for k in range(NZ):
            part = slice(k * 384, k * 384 + 384)
            store_heads(grad, (), part, position, total[:, part])


def value_gradient(position, scale, *images):
    width = images[2].shape[2]

    def image_spec(a):
        zeros = (0,) * (a.ndim - 1)
        return pl.BlockSpec((1,) + a.shape[1:], lambda i: (i,) + zeros)

    smem = pl.BlockSpec(memory_space=pltpu.SMEM)
    return pl.pallas_call(
        grad_value_kernel,
        grid=(2,),
        in_specs=[smem, smem] + [image_spec(a) for a in images],
        out_specs=pl.BlockSpec((width, 2 * HD), lambda i: (0, 0)),
        out_shape=jax.ShapeDtypeStruct((width, 2 * HD), bf16),
        scratch_shapes=[pltpu.VMEM((2 * HD, width), f32)],
        compiler_params=pltpu.CompilerParams(vmem_limit_bytes=60 * 2**20),
        cost_estimate=pl.CostEstimate(flops=10_000_000_000, bytes_accessed=10_000_000, transcendentals=0),
        name="grad_value",
    )(position, scale, *images)


def start_y(pieces, dp, y_hi, near):
    def piece(mask):
        chosen = lax.dynamic_index_in_dim(pieces, dp ^ (mask >> 1), 0, keepdims=False)
        return lax.dynamic_index_in_dim(chosen, y_hi ^ (mask & 1), 1, keepdims=False)

    return jnp.stack([piece(near), piece(1)]), piece(5 - near), piece(0)


def finish_y(came, kept, near):
    came = came.astype(f32)
    passed = (kept[0].astype(f32) + came[1]).astype(bf16)
    passed = flip(passed, Y, 5 - near, 4).astype(f32)
    return (kept[1].astype(f32) + came[0] + passed).astype(bf16)


def reduce_z(shares, z):
    result = None
    for step in range(NZ):
        piece = lax.dynamic_index_in_dim(shares, (z + step) % NZ, 1, keepdims=False)
        term = (piece if step == 0 else shift(piece, "z", step, NZ)).astype(f32)
        result = term if result is None else result + term
    return result.astype(bf16)


def body(latents, noise, timesteps, ref_errors, norm_gain, w_query, w_key, w_value, w_out):
    dp, z, y_hi = lax.axis_index("dp"), lax.axis_index("z"), lax.axis_index("yh")
    local_len, model_width = latents.shape[1], latents.shape[3]
    full_len = local_len * 8

    def head(weight, which):
        return jnp.where(which == 0, weight[:, :HD], weight[:, HD:])

    def heads(which):
        return jnp.concatenate([head(w, which) for w in (w_query, w_key, w_value, w_out.T)], axis=1)

    position = [z, dp, lax.axis_index("x"), lax.axis_index("core")]
    position = jnp.stack(position).astype(jnp.int32)
    crossed = flip(heads(1 - dp), Y, 3, 4)

    clean32 = latents[0].transpose(1, 0, 2).astype(f32)
    noise32 = noise[0].transpose(1, 0, 2).astype(f32)
    sigma = (timesteps[0].astype(f32) + 0.5) / NSTEP
    mixing = sigma[:, None, None]
    noised = ((1.0 - mixing) * clean32 + mixing * noise32).astype(bf16).astype(f32)
    target = noise32 - clean32
    inverse = lax.rsqrt(jnp.mean(noised * noised, axis=-1, keepdims=True) + norm_epsilon)
    normed = (noised * inverse * norm_gain).astype(bf16)
    normed, crossed = lax.optimization_barrier((normed, crossed))
    own, rest = gather_weight(heads(dp), crossed, y_hi)
    normed = lax.all_gather(normed, SEQ, axis=1, tiled=True)
    attended, probs, partial, blocks, out_w = forward(position, normed, own, rest)

    def columns(value, chunk):
        parts = jnp.split(value, 4, axis=2)
        return jnp.concatenate([parts[chunk], parts[2 + chunk]], axis=2)

    predicted_1 = lax.psum_scatter(partial, SEQ, scatter_dimension=1, tiled=True)
    differ_0 = sum_tokens(blocks) - columns(target, 0)
    predicted_1, differ_0 = lax.optimization_barrier((predicted_1, differ_0))
    differ_1 = predicted_1.astype(f32) - columns(target, 1)
    residual_1 = lax.all_gather(differ_1.astype(bf16), SEQ, axis=1, tiled=True)
    found = [gather_tokens(differ_0.astype(bf16)), [(residual_1,)]]
    sums = jnp.sum(differ_0 * differ_0, axis=(1, 2)) + jnp.sum(differ_1 * differ_1, axis=(1, 2))
    sums = sums + flip(sums, "core", 1, 2)
    sums = sums + flip(sums, "x", 1, 4)
    sums = sums + flip(sums, "x", 2, 4)
    errors = sums / (full_len * model_width)
    reference_pair = ref_errors[0]
    margin = errors[0] - reference_pair[0] - (errors[1] - reference_pair[1])
    pair_loss = jax.nn.softplus(preference_beta * margin)
    weight_pair = (
        preference_beta
        * jax.nn.sigmoid(preference_beta * margin)
        * 2.0
        * LOSS_SCALE
        / (full_len * model_width)
    )
    image_scale = jnp.array([1.0, -1.0], f32) * weight_pair

    def first(chunk, scale):
        grad, part = chunk_gradient(chunk, position, scale, attended, out_w, found[chunk])
        send, *kept = start_y(grad.reshape(2, 4, 2, -1, 2 * HD), dp, y_hi, 2 + chunk)
        return part, send, kept

    part_0, send_0, kept_0 = first(0, image_scale)
    came_0, scale_1 = lax.optimization_barrier((flip(send_0, Y, 2, 4), image_scale))
    part_1, send_1, kept_1 = first(1, scale_1)
    out_share_0 = finish_y(came_0, kept_0, 2)
    out_share_0, send_1, scale_2 = lax.optimization_barrier((out_share_0, send_1, scale_1))
    came_1 = flip(send_1, Y, 3, 4)
    grad_value = value_gradient(position, scale_2, part_0, part_1, normed, probs)
    grad_value, came_1 = lax.optimization_barrier((grad_value, came_1))
    pieces = grad_value.reshape(2, NZ, 2, -1, 2 * HD)
    value_shares = []
    for half in range(2):
        send, *kept = start_y(pieces[:, 4 * half : 4 * half + 4], dp, y_hi, 2 + half)
        value_shares.append(finish_y(flip(send, Y, 2 + half, 4), kept, 2 + half))
    out_shares = [out_share_0, finish_y(came_1, kept_1, 3)]
    shares = jnp.stack([jnp.concatenate(value_shares), jnp.concatenate(out_shares)])
    summed = reduce_z(shares, z)
    return summed[0], summed[1].T, pair_loss.reshape(1)


def solution(mesh):
    fine = Mesh(mesh.devices.reshape(2, NZ, 2, 4, 2), ("dp", "z", "yh", "x", "core"))
    fsdp = ("z", "yh")
    in_specs = (
        P(GROUP, SEQ, None, None),
        P(GROUP, SEQ, None, None),
        P(GROUP, None),
        P(GROUP, None),
        P(),
        P(fsdp, SEQ),
        P(fsdp, SEQ),
        P(fsdp, SEQ),
        P(SEQ, fsdp),
    )
    out_specs = (P(GROUP, SEQ), P(SEQ, GROUP), P(GROUP))
    return jax.shard_map(body, mesh=fine, in_specs=in_specs, out_specs=out_specs, check_vma=False)
```

```python
import functools
import math

import jax
import jax.numpy as jnp
from jax import lax
from jax.experimental import pallas as pl
from jax.experimental.pallas import tpu as pltpu
from jax.sharding import Mesh, PartitionSpec as P

HD = 128
NSTEP = 1000
LOSS_SCALE = 24576
NZ = 8

preference_beta = 2.0
norm_epsilon = 1e-06

SEQ = ("x", "core")
GROUP = ("dp", "z", "yh")
Y = ("dp", "yh")
bf16 = jnp.bfloat16
f32 = jnp.float32


def shift(value, axis, step, count):
    return lax.ppermute(value, axis, [(i, (i + step) % count) for i in range(count)])


def flip(value, axis, mask, count):
    return lax.ppermute(value, axis, [(i, i ^ mask) for i in range(count)])


def gather_weight(mine, crossed, y_hi):
    first = jnp.where(y_hi == 0, jnp.stack([mine, crossed]), jnp.stack([crossed, mine]))
    own, rest = {0: first}, {}

    def hand_over(keys, before=None):
        low = jnp.stack([own[k][0] for k in keys])
        high = jnp.stack([own[k][1] for k in keys])
        if before is not None:
            low, high, *_ = lax.optimization_barrier((low, high, *before))
        low, high = flip(low, Y, 2, 4), flip(high, Y, 3, 4)
        for i, k in enumerate(keys):
            rest[k] = ((low, i), (high, i))
        return low, high

    given = hand_over([0])
    right = left = first
    for step in range(1, 4):
        right = shift(right, "z", 1, NZ)
        left = shift(left, "z", NZ - 1, NZ)
        own[NZ - step], own[step] = right, left
        given = hand_over([NZ - step, step], given)
    own[4] = shift(right, "z", 1, NZ)
    hand_over([4])
    own = [((own[k], 0), (own[k], 1)) for k in range(NZ)]
    return own, [rest[k] for k in range(NZ)]


def forward_kernel(places, count, position, normed, *refs):
    weights = refs[:count]
    attended, probs, partial, out_w, qkv_w, qkv = refs[count:]
    image, tile = pl.program_id(0), pl.program_id(1)
    tile_rows = normed.shape[1]

    @pl.when((image == 0) & (tile == 0))
    def _():
        for e in range(2):
            for k in range(2 * NZ):
                which, index = places[e][k]
                block = weights[which][index]
                start = lax.rem(position[0] + k // 2, NZ) * 384 + (k % 2) * 192
                rows = pl.ds(pl.multiple_of(start, 192), 192)
                qkv_w[rows, e * 384 : e * 384 + 384] = block[:, :384]
                out_w[rows, e * HD : e * HD + HD] = block[:, 384:]

    product = jnp.dot(normed[0], qkv_w[...], preferred_element_type=f32)
    start = pl.multiple_of(tile * tile_rows, tile_rows)
    qkv[pl.ds(start, tile_rows), :] = product.astype(bf16)

    @pl.when(tile == pl.num_programs(1) - 1)
    def _():
        for e in range(2):
            base = e * 384
            query, keys = qkv[:, base : base + HD], qkv[:, base + HD : base + 2 * HD]
            scores = lax.dot_general(
                query, keys, (((1,), (1,)), ((), ())), preferred_element_type=f32
            ) * (1.0 / math.sqrt(HD))
            weight = jnp.exp(scores - jnp.max(scores, axis=-1, keepdims=True))
            prob = (weight * (1.0 / jnp.sum(weight, axis=-1, keepdims=True))).astype(bf16)
            probs[0, e] = prob
            attended[0, :, e * HD : e * HD + HD] = jnp.dot(
                prob, qkv[:, base + 2 * HD : base + 384], preferred_element_type=f32
            ).astype(bf16)
        for chunk in range(4):
            part = slice(chunk * 768, chunk * 768 + 768)
            partial[0, :, part] = lax.dot_general(
                attended[0], out_w[part, :], (((1,), (1,)), ((), ())), preferred_element_type=f32
            ).astype(bf16)


def forward(position, normed, own, rest):
    arrays, places = [], []
    for blocks in (own, rest):
        places.append([])
        for pair in blocks:
            for array, index in pair:
                known = [i for i, a in enumerate(arrays) if a is array]
                if not known:
                    arrays.append(array)
                    known = [len(arrays) - 1]
                places[-1].append((known[0], index))
    _, length, width = normed.shape
    tiles = 2
    shapes = (
        ((2, length, 2 * HD), (1, length, 2 * HD), lambda i, t: (i, 0, 0)),
        ((2, 2, length, length), (1, 2, length, length), lambda i, t: (i, 0, 0, 0)),
        ((2, length, width), (1, length, width), lambda i, t: (i, 0, 0)),
        ((width, 2 * HD), (width, 2 * HD), lambda i, t: (0, 0)),
    )
    return pl.pallas_call(
        functools.partial(forward_kernel, places, len(arrays)),
        grid=(2, tiles),
        in_specs=[
            pl.BlockSpec(memory_space=pltpu.SMEM),
            pl.BlockSpec((1, length // tiles, width), lambda i, t: (i, t, 0)),
        ]
        + [pl.BlockSpec(a.shape, lambda i, t: (0, 0, 0)) for a in arrays],
        out_specs=[pl.BlockSpec(block, index) for _, block, index in shapes],
        out_shape=[jax.ShapeDtypeStruct(shape, bf16) for shape, _, _ in shapes],
        scratch_shapes=[
            pltpu.VMEM((width, 6 * HD), bf16),
            pltpu.VMEM((length, 6 * HD), bf16),
        ],
        compiler_params=pltpu.CompilerParams(vmem_limit_bytes=60 * 2**20),
        cost_estimate=pl.CostEstimate(flops=14_000_000_000, bytes_accessed=14_000_000, transcendentals=0),
        name="forward",
    )(position, normed, *arrays)


def store_heads(grad, index, rows, position, block):
    block = block.astype(bf16)
    for e in range(2):
        column = pl.multiple_of((position[1] ^ e) * HD, HD)
        grad[index + (rows, pl.ds(column, HD))] = block[e * HD : e * HD + HD].T


def gather_tokens(own, sums):
    arrays = [shift(own, "x", 4 - offset, 4) for offset in (1, 3, 2)]
    sums = (sums + flip(sums, "x", 1, 4)) + (flip(sums, "x", 2, 4) + flip(sums, "x", 3, 4))
    found = [(own, 0, 0), (flip(own, "core", 1, 2), 0, 1)]
    arrays, sums = lax.optimization_barrier((arrays, sums))
    for array, offset in zip(arrays, (1, 3, 2)):
        found.append((array, offset, 0))
        found.append((flip(array, "core", 1, 2), offset, 1))
    return found, sums


def chunk_kernel(places, chunk, position, scale, attended, out_w, *refs):
    blocks = refs[: len(places)]
    grad, part, total = refs[len(places) : len(places) + 3]
    held = blocks[0] if places[0] is None else refs[-1]
    if places[0] is not None:
        tokens = blocks[0].shape[1]
        for block, (offset, swap) in zip(blocks, places):
            spot = lax.rem(position[2] + offset, 4) * 2 + (position[3] ^ swap)
            rows = pl.ds(pl.multiple_of(spot * tokens, tokens), tokens)
            for i in range(2):
                held[i, rows, :] = block[i]
    half = held.shape[2] // 2
    for i in range(2):
        product = None
        for owner in range(2):
            term = jnp.dot(
                held[i, :, owner * half : owner * half + half],
                out_w[owner, chunk],
                preferred_element_type=f32,
            )
            product = term if product is None else product + term
        part[i] = product
        term = jnp.dot(attended[i].T, held[i], preferred_element_type=f32) * scale[i]
        if i == 0:
            total[...] = term
        else:
            total[...] += term
    for k in range(4):
        rows = slice((k % 2) * 384, (k % 2) * 384 + 384)
        store_heads(grad, (k // 2,), rows, position, total[:, k * 384 : k * 384 + 384])


def chunk_gradient(chunk, position, scale, attended, out_w, found):
    arrays = [entry[0] for entry in found]
    places = [entry[1:] or None for entry in found]
    width = arrays[0].shape[2]
    length = attended.shape[1]
    smem = pl.BlockSpec(memory_space=pltpu.SMEM)
    vmem = pl.BlockSpec(memory_space=pltpu.VMEM)
    held = [pltpu.VMEM((2, length, width), bf16)] if places[0] else []
    return pl.pallas_call(
        functools.partial(chunk_kernel, places, chunk),
        in_specs=[smem, smem] + [vmem] * (2 + len(arrays)),
        out_specs=[vmem, vmem],
        out_shape=[
            jax.ShapeDtypeStruct((2, width // 2, 2 * HD), bf16),
            jax.ShapeDtypeStruct((2, length, 2 * HD), f32),
        ],
        scratch_shapes=[pltpu.VMEM((2 * HD, width), f32)] + held,
        compiler_params=pltpu.CompilerParams(vmem_limit_bytes=60 * 2**20),
        cost_estimate=pl.CostEstimate(
            flops=7_000_000_000, bytes_accessed=7_000_000, transcendentals=0
        ),
        name="chunk_gradient",
    )(position, scale, attended, out_w.reshape(2, 2, width // 2, 2 * HD), *arrays)


def grad_value_kernel(position, scale, part_0, part_1, normed, probs, grad, total):
    image = pl.program_id(0)
    d_attended = ((part_0[0] + part_1[0]) * scale[image]).astype(bf16)
    d_values = jnp.concatenate(
        [
            lax.dot_general(
                d_attended[:, e * HD : e * HD + HD].T, probs[0, e], (((1,), (0,)), ((), ())),
                preferred_element_type=f32,
            ).astype(bf16)
            for e in range(2)
        ],
        axis=0,
    )
    term = jnp.dot(d_values, normed[0], preferred_element_type=f32)

    @pl.when(image == 0)
    def _():
        total[...] = term

    @pl.when(image == 1)
    def _():
        total[...] += term
        for k in range(NZ):
            part = slice(k * 384, k * 384 + 384)
            store_heads(grad, (), part, position, total[:, part])


def value_gradient(position, scale, *images):
    width = images[2].shape[2]

    def image_spec(a):
        zeros = (0,) * (a.ndim - 1)
        return pl.BlockSpec((1,) + a.shape[1:], lambda i: (i,) + zeros)

    smem = pl.BlockSpec(memory_space=pltpu.SMEM)
    return pl.pallas_call(
        grad_value_kernel,
        grid=(2,),
        in_specs=[smem, smem] + [image_spec(a) for a in images],
        out_specs=pl.BlockSpec((width, 2 * HD), lambda i: (0, 0)),
        out_shape=jax.ShapeDtypeStruct((width, 2 * HD), bf16),
        scratch_shapes=[pltpu.VMEM((2 * HD, width), f32)],
        compiler_params=pltpu.CompilerParams(vmem_limit_bytes=60 * 2**20),
        cost_estimate=pl.CostEstimate(flops=10_000_000_000, bytes_accessed=10_000_000, transcendentals=0),
        name="grad_value",
    )(position, scale, *images)


def start_y(pieces, dp, y_hi, near):
    def piece(mask):
        chosen = lax.dynamic_index_in_dim(pieces, dp ^ (mask >> 1), 0, keepdims=False)
        return lax.dynamic_index_in_dim(chosen, y_hi ^ (mask & 1), 1, keepdims=False)

    return jnp.stack([piece(near), piece(1)]), piece(5 - near), piece(0)


def finish_y(came, kept, near):
    came = came.astype(f32)
    passed = (kept[0].astype(f32) + came[1]).astype(bf16)
    passed = flip(passed, Y, 5 - near, 4).astype(f32)
    return (kept[1].astype(f32) + came[0] + passed).astype(bf16)


def reduce_z(shares, z):
    result = None
    for step in range(NZ):
        piece = lax.dynamic_index_in_dim(shares, (z + step) % NZ, 1, keepdims=False)
        term = (piece if step == 0 else shift(piece, "z", step, NZ)).astype(f32)
        result = term if result is None else result + term
    return result.astype(bf16)


def body(latents, noise, timesteps, ref_errors, norm_gain, w_query, w_key, w_value, w_out):
    dp, z, y_hi = lax.axis_index("dp"), lax.axis_index("z"), lax.axis_index("yh")
    local_len, model_width = latents.shape[1], latents.shape[3]
    full_len = local_len * 8

    def head(weight, which):
        return jnp.where(which == 0, weight[:, :HD], weight[:, HD:])

    def heads(which):
        return jnp.concatenate([head(w, which) for w in (w_query, w_key, w_value, w_out.T)], axis=1)

    position = [z, dp, lax.axis_index("x"), lax.axis_index("core")]
    position = jnp.stack(position).astype(jnp.int32)
    crossed = flip(heads(1 - dp), Y, 3, 4)

    clean32 = latents[0].transpose(1, 0, 2).astype(f32)
    noise32 = noise[0].transpose(1, 0, 2).astype(f32)
    sigma = (timesteps[0].astype(f32) + 0.5) / NSTEP
    mixing = sigma[:, None, None]
    noised = ((1.0 - mixing) * clean32 + mixing * noise32).astype(bf16).astype(f32)
    target = noise32 - clean32
    inverse = lax.rsqrt(jnp.mean(noised * noised, axis=-1, keepdims=True) + norm_epsilon)
    normed = (noised * inverse * norm_gain).astype(bf16)
    normed, crossed = lax.optimization_barrier((normed, crossed))
    own, rest = gather_weight(heads(dp), crossed, y_hi)
    normed = lax.all_gather(normed, SEQ, axis=1, tiled=True)
    attended, probs, partial, out_w = forward(position, normed, own, rest)
    predicted = lax.psum_scatter(partial, SEQ, scatter_dimension=1, tiled=True).astype(f32)
    differ = predicted - target
    residual = differ.astype(bf16)
    sums = jnp.sum(differ * differ, axis=(1, 2))
    sums = sums + flip(sums, "core", 1, 2)
    residual, sums = lax.optimization_barrier((residual, sums))

    def columns(chunk):
        parts = jnp.split(residual, 4, axis=2)
        return jnp.concatenate([parts[chunk], parts[2 + chunk]], axis=2)

    residual_1 = lax.all_gather(columns(1), SEQ, axis=1, tiled=True)
    found, sums = gather_tokens(columns(0), sums)
    found = [found, [(residual_1,)]]
    errors = sums / (full_len * model_width)
    reference_pair = ref_errors[0]
    margin = errors[0] - reference_pair[0] - (errors[1] - reference_pair[1])
    pair_loss = jax.nn.softplus(preference_beta * margin)
    weight_pair = (
        preference_beta
        * jax.nn.sigmoid(preference_beta * margin)
        * 2.0
        * LOSS_SCALE
        / (full_len * model_width)
    )
    image_scale = jnp.array([1.0, -1.0], f32) * weight_pair

    def first(chunk, scale):
        grad, part = chunk_gradient(chunk, position, scale, attended, out_w, found[chunk])
        send, *kept = start_y(grad.reshape(2, 4, 2, -1, 2 * HD), dp, y_hi, 2 + chunk)
        return part, send, kept

    part_0, send_0, kept_0 = first(0, image_scale)
    send_0, scale_1 = lax.optimization_barrier((send_0, image_scale))
    came_0 = flip(send_0, Y, 2, 4)
    part_1, send_1, kept_1 = first(1, scale_1)
    send_1, scale_2 = lax.optimization_barrier((send_1, scale_1))
    came_1 = flip(send_1, Y, 3, 4)
    grad_value = value_gradient(position, scale_2, part_0, part_1, normed, probs)
    grad_value, came_0, came_1 = lax.optimization_barrier((grad_value, came_0, came_1))
    pieces = grad_value.reshape(2, NZ, 2, -1, 2 * HD)
    value_shares = []
    for half in range(2):
        send, *kept = start_y(pieces[:, 4 * half : 4 * half + 4], dp, y_hi, 2 + half)
        value_shares.append(finish_y(flip(send, Y, 2 + half, 4), kept, 2 + half))
    out_shares = [finish_y(came_0, kept_0, 2), finish_y(came_1, kept_1, 3)]
    shares = jnp.stack([jnp.concatenate(value_shares), jnp.concatenate(out_shares)])
    summed = reduce_z(shares, z)
    return summed[0], summed[1].T, pair_loss.reshape(1)


def solution(mesh):
    fine = Mesh(mesh.devices.reshape(2, NZ, 2, 4, 2), ("dp", "z", "yh", "x", "core"))
    fsdp = ("z", "yh")
    in_specs = (
        P(GROUP, SEQ, None, None),
        P(GROUP, SEQ, None, None),
        P(GROUP, None),
        P(GROUP, None),
        P(),
        P(fsdp, SEQ),
        P(fsdp, SEQ),
        P(fsdp, SEQ),
        P(SEQ, fsdp),
    )
    out_specs = (P(GROUP, SEQ), P(SEQ, GROUP), P(GROUP))
    return jax.shard_map(body, mesh=fine, in_specs=in_specs, out_specs=out_specs, check_vma=False)
```

```python
import functools
import math

import jax
import jax.numpy as jnp
from jax import lax
from jax.experimental import pallas as pl
from jax.experimental.pallas import tpu as pltpu
from jax.sharding import Mesh, PartitionSpec as P

HD = 128
NSTEP = 1000
LOSS_SCALE = 24576
NZ = 8

preference_beta = 2.0
norm_epsilon = 1e-06

SEQ = ("x", "core")
GROUP = ("dp", "z", "yh")
Y = ("dp", "yh")
bf16 = jnp.bfloat16
f32 = jnp.float32


def shift(value, axis, step, count):
    return lax.ppermute(value, axis, [(i, (i + step) % count) for i in range(count)])


def flip(value, axis, mask, count):
    return lax.ppermute(value, axis, [(i, i ^ mask) for i in range(count)])


def gather_weight(mine, crossed, y_hi):
    first = jnp.where(y_hi == 0, jnp.stack([mine, crossed]), jnp.stack([crossed, mine]))
    own, rest = {0: first}, {}

    def hand_over(keys, before=None):
        low = jnp.stack([own[k][0] for k in keys])
        high = jnp.stack([own[k][1] for k in keys])
        if before is not None:
            low, high, *_ = lax.optimization_barrier((low, high, *before))
        low, high = flip(low, Y, 2, 4), flip(high, Y, 3, 4)
        for i, k in enumerate(keys):
            rest[k] = ((low, i), (high, i))
        return low, high

    given = hand_over([0])
    right = left = first
    for step in range(1, 4):
        right = shift(right, "z", 1, NZ)
        left = shift(left, "z", NZ - 1, NZ)
        own[NZ - step], own[step] = right, left
        given = hand_over([NZ - step, step], given)
    own[4] = shift(right, "z", 1, NZ)
    hand_over([4])
    own = [((own[k], 0), (own[k], 1)) for k in range(NZ)]
    return own, [rest[k] for k in range(NZ)]


def forward_kernel(places, count, position, normed, *refs):
    weights = refs[:count]
    attended, probs, partial, out_w, qkv_w, qkv = refs[count:]
    image = pl.program_id(0)

    @pl.when(image == 0)
    def _():
        for e in range(2):
            for k in range(2 * NZ):
                which, index = places[e][k]
                block = weights[which][index]
                start = lax.rem(position[0] + k // 2, NZ) * 384 + (k % 2) * 192
                rows = pl.ds(pl.multiple_of(start, 192), 192)
                qkv_w[rows, e * 384 : e * 384 + 384] = block[:, :384]
                out_w[rows, e * HD : e * HD + HD] = block[:, 384:]

    qkv[...] = jnp.dot(normed[0], qkv_w[...], preferred_element_type=f32).astype(bf16)
    for e in range(2):
        base = e * 384
        query, keys = qkv[:, base : base + HD], qkv[:, base + HD : base + 2 * HD]
        scores = lax.dot_general(
            query, keys, (((1,), (1,)), ((), ())), preferred_element_type=f32
        ) * (1.0 / math.sqrt(HD))
        weight = jnp.exp(scores - jnp.max(scores, axis=-1, keepdims=True))
        prob = (weight * (1.0 / jnp.sum(weight, axis=-1, keepdims=True))).astype(bf16)
        probs[0, e] = prob
        attended[0, :, e * HD : e * HD + HD] = jnp.dot(
            prob, qkv[:, base + 2 * HD : base + 384], preferred_element_type=f32
        ).astype(bf16)
    for chunk in range(4):
        part = slice(chunk * 768, chunk * 768 + 768)
        partial[0, :, part] = lax.dot_general(
            attended[0], out_w[part, :], (((1,), (1,)), ((), ())), preferred_element_type=f32
        ).astype(bf16)


def forward(position, normed, own, rest):
    arrays, places = [], []
    for blocks in (own, rest):
        places.append([])
        for pair in blocks:
            for array, index in pair:
                known = [i for i, a in enumerate(arrays) if a is array]
                if not known:
                    arrays.append(array)
                    known = [len(arrays) - 1]
                places[-1].append((known[0], index))
    _, length, width = normed.shape
    shapes = (
        ((2, length, 2 * HD), (1, length, 2 * HD), lambda i: (i, 0, 0)),
        ((2, 2, length, length), (1, 2, length, length), lambda i: (i, 0, 0, 0)),
        ((2, length, width), (1, length, width), lambda i: (i, 0, 0)),
        ((width, 2 * HD), (width, 2 * HD), lambda i: (0, 0)),
    )
    return pl.pallas_call(
        functools.partial(forward_kernel, places, len(arrays)),
        grid=(2,),
        in_specs=[
            pl.BlockSpec(memory_space=pltpu.SMEM),
            pl.BlockSpec((1, length, width), lambda i: (i, 0, 0)),
        ]
        + [pl.BlockSpec(a.shape, lambda i: (0, 0, 0)) for a in arrays],
        out_specs=[pl.BlockSpec(block, index) for _, block, index in shapes],
        out_shape=[jax.ShapeDtypeStruct(shape, bf16) for shape, _, _ in shapes],
        scratch_shapes=[
            pltpu.VMEM((width, 6 * HD), bf16),
            pltpu.VMEM((length, 6 * HD), bf16),
        ],
        compiler_params=pltpu.CompilerParams(vmem_limit_bytes=60 * 2**20),
        cost_estimate=pl.CostEstimate(
            flops=14_000_000_000, bytes_accessed=14_000_000, transcendentals=0
        ),
        name="forward",
    )(position, normed, *arrays)


def store_heads(grad, index, rows, position, block):
    block = block.astype(bf16)
    for e in range(2):
        column = pl.multiple_of((position[1] ^ e) * HD, HD)
        grad[index + (rows, pl.ds(column, HD))] = block[e * HD : e * HD + HD].T


def gather_tokens(own, sums):
    arrays = [shift(own, "x", 4 - offset, 4) for offset in (1, 3, 2)]
    sums = (sums + flip(sums, "x", 1, 4)) + (flip(sums, "x", 2, 4) + flip(sums, "x", 3, 4))
    found = [(own, 0, 0), (flip(own, "core", 1, 2), 0, 1)]
    arrays, sums = lax.optimization_barrier((arrays, sums))
    for array, offset in zip(arrays, (1, 3, 2)):
        found.append((array, offset, 0))
        found.append((flip(array, "core", 1, 2), offset, 1))
    return found, sums


def chunk_kernel(places, chunk, position, scale, attended, out_w, *refs):
    blocks = refs[: len(places)]
    grad, part, total = refs[len(places) : len(places) + 3]
    held = blocks[0] if places[0] is None else refs[-1]
    if places[0] is not None:
        tokens = blocks[0].shape[1]
        for block, (offset, swap) in zip(blocks, places):
            spot = lax.rem(position[2] + offset, 4) * 2 + (position[3] ^ swap)
            rows = pl.ds(pl.multiple_of(spot * tokens, tokens), tokens)
            for i in range(2):
                held[i, rows, :] = block[i]
    half = held.shape[2] // 2
    for i in range(2):
        product = None
        for owner in range(2):
            term = jnp.dot(
                held[i, :, owner * half : owner * half + half],
                out_w[owner, chunk],
                preferred_element_type=f32,
            )
            product = term if product is None else product + term
        part[i] = product
        term = jnp.dot(attended[i].T, held[i], preferred_element_type=f32) * scale[i]
        if i == 0:
            total[...] = term
        else:
            total[...] += term
    for k in range(4):
        rows = slice((k % 2) * 384, (k % 2) * 384 + 384)
        store_heads(grad, (k // 2,), rows, position, total[:, k * 384 : k * 384 + 384])


def chunk_gradient(chunk, position, scale, attended, out_w, found):
    arrays = [entry[0] for entry in found]
    places = [entry[1:] or None for entry in found]
    width = arrays[0].shape[2]
    length = attended.shape[1]
    smem = pl.BlockSpec(memory_space=pltpu.SMEM)
    vmem = pl.BlockSpec(memory_space=pltpu.VMEM)
    held = [pltpu.VMEM((2, length, width), bf16)] if places[0] else []
    return pl.pallas_call(
        functools.partial(chunk_kernel, places, chunk),
        in_specs=[smem, smem] + [vmem] * (2 + len(arrays)),
        out_specs=[vmem, vmem],
        out_shape=[
            jax.ShapeDtypeStruct((2, width // 2, 2 * HD), bf16),
            jax.ShapeDtypeStruct((2, length, 2 * HD), f32),
        ],
        scratch_shapes=[pltpu.VMEM((2 * HD, width), f32)] + held,
        compiler_params=pltpu.CompilerParams(vmem_limit_bytes=60 * 2**20),
        cost_estimate=pl.CostEstimate(
            flops=7_000_000_000, bytes_accessed=7_000_000, transcendentals=0
        ),
        name="chunk_gradient",
    )(position, scale, attended, out_w.reshape(2, 2, width // 2, 2 * HD), *arrays)


def value_kernel(chunk, position, scale, *refs):
    owner, image = pl.program_id(0), pl.program_id(1)
    if chunk == 0:
        part_0, part_1, probs, normed, grad, d_values, total = refs

        @pl.when(owner == 0)
        def _():
            d_attended = ((part_0[0] + part_1[0]) * scale[image]).astype(bf16)
            for e in range(2):
                d_values[image, e * HD : e * HD + HD, :] = lax.dot_general(
                    d_attended[:, e * HD : e * HD + HD].T,
                    probs[0, e],
                    (((1,), (0,)), ((), ())),
                    preferred_element_type=f32,
                ).astype(bf16)
    else:
        d_values, normed, grad, total = refs
    term = jnp.dot(d_values[image], normed[0], preferred_element_type=f32)

    @pl.when(image == 0)
    def _():
        total[...] = term

    @pl.when(image == 1)
    def _():
        total[...] += term
        for k in range(2):
            rows = slice(k * 384, k * 384 + 384)
            store_heads(grad, (0,), rows, position, total[:, rows])


def value_gradient(chunk, position, scale, *arrays):
    _, length, width = arrays[-1].shape
    half = width // 4
    smem = pl.BlockSpec(memory_space=pltpu.SMEM)

    def once(a):
        zeros = (0,) * (a.ndim - 1)
        return pl.BlockSpec((1,) + a.shape[1:], lambda o, i: (lax.max(o, i),) + zeros)

    whole = pl.BlockSpec((2, 2 * HD, length), lambda o, i: (0, 0, 0))
    normed_spec = pl.BlockSpec((1, length, half), lambda o, i: (i, 0, 2 * o + chunk))
    shapes = [(2, half, 2 * HD), (2, 2 * HD, length)][: 2 - chunk]
    out_specs = [pl.BlockSpec((1, half, 2 * HD), lambda o, i: (o, 0, 0)), whole][: 2 - chunk]
    specs = [once(a) for a in arrays[:-1]] if chunk == 0 else [whole]
    return pl.pallas_call(
        functools.partial(value_kernel, chunk),
        grid=(2, 2),
        in_specs=[smem, smem] + specs + [normed_spec],
        out_specs=out_specs,
        out_shape=[jax.ShapeDtypeStruct(shape, bf16) for shape in shapes],
        scratch_shapes=[pltpu.VMEM((2 * HD, half), f32)],
        compiler_params=pltpu.CompilerParams(vmem_limit_bytes=60 * 2**20),
        cost_estimate=pl.CostEstimate(
            flops=5_000_000_000, bytes_accessed=5_000_000, transcendentals=0
        ),
        name="grad_value",
    )(position, scale, *arrays)


def start_y(pieces, dp, y_hi, near):
    def piece(mask):
        chosen = lax.dynamic_index_in_dim(pieces, dp ^ (mask >> 1), 0, keepdims=False)
        return lax.dynamic_index_in_dim(chosen, y_hi ^ (mask & 1), 1, keepdims=False)

    return jnp.stack([piece(near), piece(1)]), piece(5 - near), piece(0)


def finish_y(came, kept, near):
    came = came.astype(f32)
    passed = (kept[0].astype(f32) + came[1]).astype(bf16)
    passed = flip(passed, Y, 5 - near, 4).astype(f32)
    return (kept[1].astype(f32) + came[0] + passed).astype(bf16)


def reduce_z(shares):
    shares = lax.all_to_all(shares, "z", 0, 0, tiled=True)
    return sum(shares[i].astype(f32) for i in range(NZ)).astype(bf16)


def body(latents, noise, timesteps, ref_errors, norm_gain, w_query, w_key, w_value, w_out):
    dp, z, y_hi = lax.axis_index("dp"), lax.axis_index("z"), lax.axis_index("yh")
    local_len, model_width = latents.shape[1], latents.shape[3]
    full_len = local_len * 8

    def head(weight, which):
        return jnp.where(which == 0, weight[:, :HD], weight[:, HD:])

    def heads(which):
        return jnp.concatenate([head(w, which) for w in (w_query, w_key, w_value, w_out.T)], axis=1)

    position = [z, dp, lax.axis_index("x"), lax.axis_index("core")]
    position = jnp.stack(position).astype(jnp.int32)
    crossed = flip(heads(1 - dp), Y, 3, 4)

    clean32 = latents[0].transpose(1, 0, 2).astype(f32)
    noise32 = noise[0].transpose(1, 0, 2).astype(f32)
    sigma = (timesteps[0].astype(f32) + 0.5) / NSTEP
    mixing = sigma[:, None, None]
    noised = ((1.0 - mixing) * clean32 + mixing * noise32).astype(bf16).astype(f32)
    target = noise32 - clean32
    inverse = lax.rsqrt(jnp.mean(noised * noised, axis=-1, keepdims=True) + norm_epsilon)
    normed = (noised * inverse * norm_gain).astype(bf16)
    normed, crossed = lax.optimization_barrier((normed, crossed))
    own, rest = gather_weight(heads(dp), crossed, y_hi)
    normed = lax.all_gather(normed, SEQ, axis=1, tiled=True)
    attended, probs, partial, out_w = forward(position, normed, own, rest)
    predicted = lax.psum_scatter(partial, SEQ, scatter_dimension=1, tiled=True).astype(f32)
    differ = predicted - target
    residual = differ.astype(bf16)
    sums = jnp.sum(differ * differ, axis=(1, 2))
    sums = sums + flip(sums, "core", 1, 2)
    residual, sums = lax.optimization_barrier((residual, sums))

    def columns(chunk):
        parts = jnp.split(residual, 4, axis=2)
        return jnp.concatenate([parts[chunk], parts[2 + chunk]], axis=2)

    residual_1 = lax.all_gather(columns(1), SEQ, axis=1, tiled=True)
    found, sums = gather_tokens(columns(0), sums)
    found = [found, [(residual_1,)]]
    errors = sums / (full_len * model_width)
    reference_pair = ref_errors[0]
    margin = errors[0] - reference_pair[0] - (errors[1] - reference_pair[1])
    pair_loss = jax.nn.softplus(preference_beta * margin)
    weight_pair = (
        preference_beta
        * jax.nn.sigmoid(preference_beta * margin)
        * 2.0
        * LOSS_SCALE
        / (full_len * model_width)
    )
    image_scale = jnp.array([1.0, -1.0], f32) * weight_pair

    def first(chunk, scale):
        grad, part = chunk_gradient(chunk, position, scale, attended, out_w, found[chunk])
        send, *kept = start_y(grad.reshape(2, 4, 2, -1, 2 * HD), dp, y_hi, 2 + chunk)
        return part, send, kept

    part_0, send_0, kept_0 = first(0, image_scale)
    send_0, scale_1 = lax.optimization_barrier((send_0, image_scale))
    came_0 = flip(send_0, Y, 2, 4)
    part_1, send_1, kept_1 = first(1, scale_1)
    send_1, scale_2 = lax.optimization_barrier((send_1, scale_1))
    came_1 = flip(send_1, Y, 3, 4)
    grad_0, d_values = value_gradient(0, position, scale_2, part_0, part_1, probs, normed)
    sent_0, *left_0 = start_y(grad_0.reshape(2, 4, 2, -1, 2 * HD), dp, y_hi, 2)
    sent_0, d_values, came_0 = lax.optimization_barrier((sent_0, d_values, came_0))
    back_0 = flip(sent_0, Y, 2, 4)
    (grad_1,) = value_gradient(1, position, scale_2, d_values, normed)
    sent_1, *left_1 = start_y(grad_1.reshape(2, 4, 2, -1, 2 * HD), dp, y_hi, 3)
    sent_1, came_1 = lax.optimization_barrier((sent_1, came_1))
    back_1 = flip(sent_1, Y, 3, 4)
    out_shares = [finish_y(came_0, kept_0, 2), finish_y(came_1, kept_1, 3)]
    value_shares = [finish_y(back_0, left_0, 2), finish_y(back_1, left_1, 3)]
    grad_out = reduce_z(jnp.concatenate(out_shares))
    grad_value = reduce_z(jnp.concatenate(value_shares))
    return grad_value, grad_out.T, pair_loss.reshape(1)


def solution(mesh):
    fine = Mesh(mesh.devices.reshape(2, NZ, 2, 4, 2), ("dp", "z", "yh", "x", "core"))
    fsdp = ("z", "yh")
    in_specs = (
        P(GROUP, SEQ, None, None),
        P(GROUP, SEQ, None, None),
        P(GROUP, None),
        P(GROUP, None),
        P(),
        P(fsdp, SEQ),
        P(fsdp, SEQ),
        P(fsdp, SEQ),
        P(SEQ, fsdp),
    )
    out_specs = (P(GROUP, SEQ), P(SEQ, GROUP), P(GROUP))
    return jax.shard_map(body, mesh=fine, in_specs=in_specs, out_specs=out_specs, check_vma=False)
```

```python
import functools
import math

import jax
import jax.numpy as jnp
from jax import lax
from jax.experimental import pallas as pl
from jax.experimental.pallas import tpu as pltpu
from jax.sharding import Mesh, PartitionSpec as P

HD = 128
NSTEP = 1000
LOSS_SCALE = 24576
NZ = 8

preference_beta = 2.0
norm_epsilon = 1e-06

SEQ = ("x", "core")
GROUP = ("dp", "z", "yh")
Y = ("dp", "yh")
bf16 = jnp.bfloat16
f32 = jnp.float32


def shift(value, axis, step, count):
    return lax.ppermute(value, axis, [(i, (i + step) % count) for i in range(count)])


def flip(value, axis, mask, count):
    return lax.ppermute(value, axis, [(i, i ^ mask) for i in range(count)])


def gather_weight(mine, crossed, y_hi):
    first = jnp.where(y_hi == 0, jnp.stack([mine, crossed]), jnp.stack([crossed, mine]))
    own, rest = {0: first}, {}

    def hand_over(keys, before=None):
        low = jnp.stack([own[k][0] for k in keys])
        high = jnp.stack([own[k][1] for k in keys])
        if before is not None:
            low, high, *_ = lax.optimization_barrier((low, high, *before))
        low, high = flip(low, Y, 2, 4), flip(high, Y, 3, 4)
        for i, k in enumerate(keys):
            rest[k] = ((low, i), (high, i))
        return low, high

    given = hand_over([0])
    right = left = first
    for step in range(1, 4):
        right = shift(right, "z", 1, NZ)
        left = shift(left, "z", NZ - 1, NZ)
        own[NZ - step], own[step] = right, left
        given = hand_over([NZ - step, step], given)
    own[4] = shift(right, "z", 1, NZ)
    hand_over([4])
    own = [((own[k], 0), (own[k], 1)) for k in range(NZ)]
    return own, [rest[k] for k in range(NZ)]


def forward_kernel(places, count, position, normed, *refs):
    weights = refs[:count]
    attended, probs, partial, out_w, qkv_w, qkv = refs[count:]
    image = pl.program_id(0)

    @pl.when(image == 0)
    def _():
        for e in range(2):
            for k in range(2 * NZ):
                which, index = places[e][k]
                block = weights[which][index]
                start = lax.rem(position[0] + k // 2, NZ) * 384 + (k % 2) * 192
                rows = pl.ds(pl.multiple_of(start, 192), 192)
                qkv_w[rows, e * 384 : e * 384 + 384] = block[:, :384]
                out_w[rows, e * HD : e * HD + HD] = block[:, 384:]

    qkv[...] = jnp.dot(normed[0], qkv_w[...], preferred_element_type=f32).astype(bf16)
    for e in range(2):
        base = e * 384
        query, keys = qkv[:, base : base + HD], qkv[:, base + HD : base + 2 * HD]
        scores = lax.dot_general(
            query, keys, (((1,), (1,)), ((), ())), preferred_element_type=f32
        ) * (1.0 / math.sqrt(HD))
        weight = jnp.exp(scores - jnp.max(scores, axis=-1, keepdims=True))
        prob = (weight * (1.0 / jnp.sum(weight, axis=-1, keepdims=True))).astype(bf16)
        probs[0, e] = prob
        attended[0, :, e * HD : e * HD + HD] = jnp.dot(
            prob, qkv[:, base + 2 * HD : base + 384], preferred_element_type=f32
        ).astype(bf16)
    for chunk in range(4):
        part = slice(chunk * 768, chunk * 768 + 768)
        partial[0, :, part] = lax.dot_general(
            attended[0], out_w[part, :], (((1,), (1,)), ((), ())), preferred_element_type=f32
        ).astype(bf16)


def forward(position, normed, own, rest):
    arrays, places = [], []
    for blocks in (own, rest):
        places.append([])
        for pair in blocks:
            for array, index in pair:
                known = [i for i, a in enumerate(arrays) if a is array]
                if not known:
                    arrays.append(array)
                    known = [len(arrays) - 1]
                places[-1].append((known[0], index))
    _, length, width = normed.shape
    shapes = (
        ((2, length, 2 * HD), (1, length, 2 * HD), lambda i: (i, 0, 0)),
        ((2, 2, length, length), (1, 2, length, length), lambda i: (i, 0, 0, 0)),
        ((2, length, width), (1, length, width), lambda i: (i, 0, 0)),
        ((width, 2 * HD), (width, 2 * HD), lambda i: (0, 0)),
    )
    return pl.pallas_call(
        functools.partial(forward_kernel, places, len(arrays)),
        grid=(2,),
        in_specs=[
            pl.BlockSpec(memory_space=pltpu.SMEM),
            pl.BlockSpec((1, length, width), lambda i: (i, 0, 0)),
        ]
        + [pl.BlockSpec(a.shape, lambda i: (0, 0, 0)) for a in arrays],
        out_specs=[pl.BlockSpec(block, index) for _, block, index in shapes],
        out_shape=[jax.ShapeDtypeStruct(shape, bf16) for shape, _, _ in shapes],
        scratch_shapes=[
            pltpu.VMEM((width, 6 * HD), bf16),
            pltpu.VMEM((length, 6 * HD), bf16),
        ],
        compiler_params=pltpu.CompilerParams(vmem_limit_bytes=60 * 2**20),
        cost_estimate=pl.CostEstimate(
            flops=14_000_000_000, bytes_accessed=14_000_000, transcendentals=0
        ),
        name="forward",
    )(position, normed, *arrays)


def store_heads(grad, index, rows, position, block):
    block = block.astype(bf16)
    for e in range(2):
        column = pl.multiple_of((position[1] ^ e) * HD, HD)
        grad[index + (rows, pl.ds(column, HD))] = block[e * HD : e * HD + HD].T


def gather_tokens(own, left, right):
    far_0 = shift(left[0:1], "x", 1, 4)
    far_1 = shift(right[1:2], "x", 3, 4)
    found = []
    for array, image, offset in (
        (own, None, 0), (left, None, 3), (right, None, 1), (far_0, 0, 2), (far_1, 1, 2)
    ):
        found.append((array, image, offset, 0))
        found.append((flip(array, "core", 1, 2), image, offset, 1))
    return found


def chunk_kernel(places, chunk, position, scale, attended, out_w, *refs):
    blocks = refs[: len(places)]
    grad, part, total = refs[len(places) : len(places) + 3]
    held = refs[-1]
    tokens = blocks[0].shape[1]
    for block, (image, offset, swap) in zip(blocks, places):
        spot = lax.rem(position[2] + offset, 4) * 2 + (position[3] ^ swap)
        rows = pl.ds(pl.multiple_of(spot * tokens, tokens), tokens)
        for i in range(2) if image is None else (image,):
            held[i, rows, :] = block[i if image is None else 0]
    half = held.shape[2] // 2
    for i in range(2):
        product = None
        for owner in range(2):
            term = jnp.dot(
                held[i, :, owner * half : owner * half + half],
                out_w[owner, chunk],
                preferred_element_type=f32,
            )
            product = term if product is None else product + term
        part[i] = product
        term = jnp.dot(attended[i].T, held[i], preferred_element_type=f32) * scale[i]
        if i == 0:
            total[...] = term
        else:
            total[...] += term
    for k in range(4):
        rows = slice((k % 2) * 384, (k % 2) * 384 + 384)
        store_heads(grad, (k // 2,), rows, position, total[:, k * 384 : k * 384 + 384])


def chunk_gradient(chunk, position, scale, attended, out_w, found):
    arrays = [entry[0] for entry in found]
    places = [entry[1:] for entry in found]
    width = arrays[0].shape[2]
    length = attended.shape[1]
    smem = pl.BlockSpec(memory_space=pltpu.SMEM)
    vmem = pl.BlockSpec(memory_space=pltpu.VMEM)
    return pl.pallas_call(
        functools.partial(chunk_kernel, places, chunk),
        in_specs=[smem, smem] + [vmem] * (2 + len(arrays)),
        out_specs=[vmem, vmem],
        out_shape=[
            jax.ShapeDtypeStruct((2, width // 2, 2 * HD), bf16),
            jax.ShapeDtypeStruct((2, length, 2 * HD), f32),
        ],
        scratch_shapes=[pltpu.VMEM((2 * HD, width), f32), pltpu.VMEM((2, length, width), bf16)],
        compiler_params=pltpu.CompilerParams(vmem_limit_bytes=60 * 2**20),
        cost_estimate=pl.CostEstimate(
            flops=7_000_000_000, bytes_accessed=7_000_000, transcendentals=0
        ),
        name="chunk_gradient",
    )(position, scale, attended, out_w.reshape(2, 2, width // 2, 2 * HD), *arrays)


def grad_value_kernel(position, scale, part_0, part_1, normed, probs, grad, total):
    image = pl.program_id(0)
    d_attended = ((part_0[0] + part_1[0]) * scale[image]).astype(bf16)
    d_values = jnp.concatenate(
        [
            lax.dot_general(
                d_attended[:, e * HD : e * HD + HD].T, probs[0, e], (((1,), (0,)), ((), ())),
                preferred_element_type=f32,
            ).astype(bf16)
            for e in range(2)
        ],
        axis=0,
    )
    term = jnp.dot(d_values, normed[0], preferred_element_type=f32)

    @pl.when(image == 0)
    def _():
        total[...] = term

    @pl.when(image == 1)
    def _():
        total[...] += term
        for k in range(NZ):
            part = slice(k * 384, k * 384 + 384)
            store_heads(grad, (), part, position, total[:, part])


def value_gradient(position, scale, *images):
    width = images[2].shape[2]

    def image_spec(a):
        zeros = (0,) * (a.ndim - 1)
        return pl.BlockSpec((1,) + a.shape[1:], lambda i: (i,) + zeros)

    smem = pl.BlockSpec(memory_space=pltpu.SMEM)
    return pl.pallas_call(
        grad_value_kernel,
        grid=(2,),
        in_specs=[smem, smem] + [image_spec(a) for a in images],
        out_specs=pl.BlockSpec((width, 2 * HD), lambda i: (0, 0)),
        out_shape=jax.ShapeDtypeStruct((width, 2 * HD), bf16),
        scratch_shapes=[pltpu.VMEM((2 * HD, width), f32)],
        compiler_params=pltpu.CompilerParams(vmem_limit_bytes=60 * 2**20),
        cost_estimate=pl.CostEstimate(flops=10_000_000_000, bytes_accessed=10_000_000, transcendentals=0),
        name="grad_value",
    )(position, scale, *images)


def start_y(pieces, dp, y_hi, near):
    def piece(mask):
        chosen = lax.dynamic_index_in_dim(pieces, dp ^ (mask >> 1), 0, keepdims=False)
        return lax.dynamic_index_in_dim(chosen, y_hi ^ (mask & 1), 1, keepdims=False)

    return jnp.stack([piece(near), piece(1)]), piece(5 - near), piece(0)


def finish_y(came, kept, near):
    came = came.astype(f32)
    passed = (kept[0].astype(f32) + came[1]).astype(bf16)
    passed = flip(passed, Y, 5 - near, 4).astype(f32)
    return (kept[1].astype(f32) + came[0] + passed).astype(bf16)


def reduce_z(shares):
    shares = lax.all_to_all(shares, "z", 0, 0, tiled=True)
    return sum(shares[i].astype(f32) for i in range(NZ)).astype(bf16)


def body(latents, noise, timesteps, ref_errors, norm_gain, w_query, w_key, w_value, w_out):
    dp, z, y_hi = lax.axis_index("dp"), lax.axis_index("z"), lax.axis_index("yh")
    local_len, model_width = latents.shape[1], latents.shape[3]
    full_len = local_len * 8

    def head(weight, which):
        return jnp.where(which == 0, weight[:, :HD], weight[:, HD:])

    def heads(which):
        return jnp.concatenate([head(w, which) for w in (w_query, w_key, w_value, w_out.T)], axis=1)

    position = [z, dp, lax.axis_index("x"), lax.axis_index("core")]
    position = jnp.stack(position).astype(jnp.int32)
    crossed = flip(heads(1 - dp), Y, 3, 4)

    clean32 = latents[0].transpose(1, 0, 2).astype(f32)
    noise32 = noise[0].transpose(1, 0, 2).astype(f32)
    sigma = (timesteps[0].astype(f32) + 0.5) / NSTEP
    mixing = sigma[:, None, None]
    noised = ((1.0 - mixing) * clean32 + mixing * noise32).astype(bf16).astype(f32)
    target = noise32 - clean32
    inverse = lax.rsqrt(jnp.mean(noised * noised, axis=-1, keepdims=True) + norm_epsilon)
    normed = (noised * inverse * norm_gain).astype(bf16)
    normed, crossed = lax.optimization_barrier((normed, crossed))
    own, rest = gather_weight(heads(dp), crossed, y_hi)
    normed = lax.all_gather(normed, SEQ, axis=1, tiled=True)
    attended, probs, partial, out_w = forward(position, normed, own, rest)
    predicted = lax.psum_scatter(partial, SEQ, scatter_dimension=1, tiled=True).astype(f32)
    differ = predicted - target
    residual = differ.astype(bf16)
    sums = jnp.sum(differ * differ, axis=(1, 2))
    sums = sums + flip(sums, "core", 1, 2)
    residual, sums = lax.optimization_barrier((residual, sums))

    def columns(chunk):
        parts = jnp.split(residual, 4, axis=2)
        return jnp.concatenate([parts[chunk], parts[2 + chunk]], axis=2)

    own_0, own_1 = columns(0), columns(1)
    left_0, right_0 = shift(own_0, "x", 1, 4), shift(own_0, "x", 3, 4)
    sums = (sums + flip(sums, "x", 1, 4)) + (flip(sums, "x", 2, 4) + flip(sums, "x", 3, 4))
    left_0, right_0, sums, own_1 = lax.optimization_barrier((left_0, right_0, sums, own_1))
    left_1, right_1 = shift(own_1, "x", 1, 4), shift(own_1, "x", 3, 4)
    found = [gather_tokens(own_0, left_0, right_0), gather_tokens(own_1, left_1, right_1)]
    errors = sums / (full_len * model_width)
    reference_pair = ref_errors[0]
    margin = errors[0] - reference_pair[0] - (errors[1] - reference_pair[1])
    pair_loss = jax.nn.softplus(preference_beta * margin)
    weight_pair = (
        preference_beta
        * jax.nn.sigmoid(preference_beta * margin)
        * 2.0
        * LOSS_SCALE
        / (full_len * model_width)
    )
    image_scale = jnp.array([1.0, -1.0], f32) * weight_pair

    def first(chunk, scale):
        grad, part = chunk_gradient(chunk, position, scale, attended, out_w, found[chunk])
        send, *kept = start_y(grad.reshape(2, 4, 2, -1, 2 * HD), dp, y_hi, 2 + chunk)
        return part, send, kept

    part_0, send_0, kept_0 = first(0, image_scale)
    send_0, scale_1 = lax.optimization_barrier((send_0, image_scale))
    came_0 = flip(send_0, Y, 2, 4)
    part_1, send_1, kept_1 = first(1, scale_1)
    send_1, scale_2 = lax.optimization_barrier((send_1, scale_1))
    came_1 = flip(send_1, Y, 3, 4)
    grad_value = value_gradient(position, scale_2, part_0, part_1, normed, probs)
    grad_value, came_0, came_1 = lax.optimization_barrier((grad_value, came_0, came_1))
    pieces = grad_value.reshape(2, NZ, 2, -1, 2 * HD)
    value_shares = []
    for half in range(2):
        send, *kept = start_y(pieces[:, 4 * half : 4 * half + 4], dp, y_hi, 2 + half)
        value_shares.append(finish_y(flip(send, Y, 2 + half, 4), kept, 2 + half))
    out_shares = [finish_y(came_0, kept_0, 2), finish_y(came_1, kept_1, 3)]
    shares = jnp.stack([jnp.concatenate(value_shares), jnp.concatenate(out_shares)], axis=1)
    summed = reduce_z(shares)
    return summed[0], summed[1].T, pair_loss.reshape(1)


def solution(mesh):
    fine = Mesh(mesh.devices.reshape(2, NZ, 2, 4, 2), ("dp", "z", "yh", "x", "core"))
    fsdp = ("z", "yh")
    in_specs = (
        P(GROUP, SEQ, None, None),
        P(GROUP, SEQ, None, None),
        P(GROUP, None),
        P(GROUP, None),
        P(),
        P(fsdp, SEQ),
        P(fsdp, SEQ),
        P(fsdp, SEQ),
        P(SEQ, fsdp),
    )
    out_specs = (P(GROUP, SEQ), P(SEQ, GROUP), P(GROUP))
    return jax.shard_map(body, mesh=fine, in_specs=in_specs, out_specs=out_specs, check_vma=False)
```

```python
import functools
import math

import jax
import jax.numpy as jnp
from jax import lax
from jax.experimental import pallas as pl
from jax.experimental.pallas import tpu as pltpu
from jax.sharding import Mesh, PartitionSpec as P

HD = 128
NSTEP = 1000
LOSS_SCALE = 24576
NZ = 8

preference_beta = 2.0
norm_epsilon = 1e-06

SEQ = ("x", "core")
GROUP = ("dp", "z", "yh")
Y = ("dp", "yh")
bf16 = jnp.bfloat16
f32 = jnp.float32


def shift(value, axis, step, count):
    return lax.ppermute(value, axis, [(i, (i + step) % count) for i in range(count)])


def flip(value, axis, mask, count):
    return lax.ppermute(value, axis, [(i, i ^ mask) for i in range(count)])


def gather_weight(mine, crossed, y_hi):
    first = jnp.where(y_hi == 0, jnp.stack([mine, crossed]), jnp.stack([crossed, mine]))
    own, rest = {0: first}, {}

    def hand_over(keys, before=None):
        low = jnp.stack([own[k][0] for k in keys])
        high = jnp.stack([own[k][1] for k in keys])
        if before is not None:
            low, high, *_ = lax.optimization_barrier((low, high, *before))
        low, high = flip(low, Y, 2, 4), flip(high, Y, 3, 4)
        for i, k in enumerate(keys):
            rest[k] = ((low, i), (high, i))
        return low, high

    given = hand_over([0])
    right = left = first
    for step in range(1, 4):
        right = shift(right, "z", 1, NZ)
        left = shift(left, "z", NZ - 1, NZ)
        own[NZ - step], own[step] = right, left
        given = hand_over([NZ - step, step], given)
    own[4] = shift(right, "z", 1, NZ)
    hand_over([4])
    own = [((own[k], 0), (own[k], 1)) for k in range(NZ)]
    return own, [rest[k] for k in range(NZ)]


def forward_kernel(places, count, position, normed, *refs):
    weights = refs[:count]
    attended, probs, partial, out_w, qkv_w, qkv = refs[count:]
    image = pl.program_id(0)

    @pl.when(image == 0)
    def _():
        for e in range(2):
            for k in range(2 * NZ):
                which, index = places[e][k]
                block = weights[which][index]
                start = lax.rem(position[0] + k // 2, NZ) * 384 + (k % 2) * 192
                rows = pl.ds(pl.multiple_of(start, 192), 192)
                qkv_w[rows, e * 384 : e * 384 + 384] = block[:, :384]
                out_w[rows, e * HD : e * HD + HD] = block[:, 384:]

    qkv[...] = jnp.dot(normed[0], qkv_w[...], preferred_element_type=f32).astype(bf16)
    for e in range(2):
        base = e * 384
        query, keys = qkv[:, base : base + HD], qkv[:, base + HD : base + 2 * HD]
        scores = lax.dot_general(
            query, keys, (((1,), (1,)), ((), ())), preferred_element_type=f32
        ) * (1.0 / math.sqrt(HD))
        weight = jnp.exp(scores - jnp.max(scores, axis=-1, keepdims=True))
        prob = (weight * (1.0 / jnp.sum(weight, axis=-1, keepdims=True))).astype(bf16)
        probs[0, e] = prob
        attended[0, :, e * HD : e * HD + HD] = jnp.dot(
            prob, qkv[:, base + 2 * HD : base + 384], preferred_element_type=f32
        ).astype(bf16)
    for chunk in range(4):
        part = slice(chunk * 768, chunk * 768 + 768)
        partial[0, :, part] = lax.dot_general(
            attended[0], out_w[part, :], (((1,), (1,)), ((), ())), preferred_element_type=f32
        ).astype(bf16)


def forward(position, normed, own, rest):
    arrays, places = [], []
    for blocks in (own, rest):
        places.append([])
        for pair in blocks:
            for array, index in pair:
                known = [i for i, a in enumerate(arrays) if a is array]
                if not known:
                    arrays.append(array)
                    known = [len(arrays) - 1]
                places[-1].append((known[0], index))
    _, length, width = normed.shape
    shapes = (
        ((2, length, 2 * HD), (1, length, 2 * HD), lambda i: (i, 0, 0)),
        ((2, 2, length, length), (1, 2, length, length), lambda i: (i, 0, 0, 0)),
        ((2, length, width), (1, length, width), lambda i: (i, 0, 0)),
        ((width, 2 * HD), (width, 2 * HD), lambda i: (0, 0)),
    )
    return pl.pallas_call(
        functools.partial(forward_kernel, places, len(arrays)),
        grid=(2,),
        in_specs=[
            pl.BlockSpec(memory_space=pltpu.SMEM),
            pl.BlockSpec((1, length, width), lambda i: (i, 0, 0)),
        ]
        + [pl.BlockSpec(a.shape, lambda i: (0, 0, 0)) for a in arrays],
        out_specs=[pl.BlockSpec(block, index) for _, block, index in shapes],
        out_shape=[jax.ShapeDtypeStruct(shape, bf16) for shape, _, _ in shapes],
        scratch_shapes=[
            pltpu.VMEM((width, 6 * HD), bf16),
            pltpu.VMEM((length, 6 * HD), bf16),
        ],
        compiler_params=pltpu.CompilerParams(vmem_limit_bytes=60 * 2**20),
        cost_estimate=pl.CostEstimate(
            flops=14_000_000_000, bytes_accessed=14_000_000, transcendentals=0
        ),
        name="forward",
    )(position, normed, *arrays)


def store_heads(grad, index, rows, position, block):
    block = block.astype(bf16)
    for e in range(2):
        column = pl.multiple_of((position[1] ^ e) * HD, HD)
        grad[index + (rows, pl.ds(column, HD))] = block[e * HD : e * HD + HD].T


def gather_tokens(own):
    arrays = {offset: shift(own, "x", 4 - offset, 4) for offset in (1, 3, 2)}
    found = [(own, 0, 0), (flip(own, "core", 1, 2), 0, 1)]
    for offset, array in arrays.items():
        found.append((array, offset, 0))
        found.append((flip(array, "core", 1, 2), offset, 1))
    return found


def chunk_kernel(places, chunk, position, scale, attended, out_w, *refs):
    blocks = refs[: len(places)]
    grad, part, total = refs[len(places) : len(places) + 3]
    held = blocks[0] if places[0] is None else refs[-1]
    if places[0] is not None:
        tokens = blocks[0].shape[1]
        for block, (offset, swap) in zip(blocks, places):
            spot = lax.rem(position[2] + offset, 4) * 2 + (position[3] ^ swap)
            rows = pl.ds(pl.multiple_of(spot * tokens, tokens), tokens)
            for i in range(2):
                held[i, rows, :] = block[i]
    half = held.shape[2] // 2
    for i in range(2):
        product = None
        for owner in range(2):
            term = jnp.dot(
                held[i, :, owner * half : owner * half + half],
                out_w[owner, chunk],
                preferred_element_type=f32,
            )
            product = term if product is None else product + term
        part[i] = product
        term = jnp.dot(attended[i].T, held[i], preferred_element_type=f32) * scale[i]
        if i == 0:
            total[...] = term
        else:
            total[...] += term
    for k in range(4):
        rows = slice((k % 2) * 384, (k % 2) * 384 + 384)
        store_heads(grad, (k // 2,), rows, position, total[:, k * 384 : k * 384 + 384])


def chunk_gradient(chunk, position, scale, attended, out_w, found):
    arrays = [entry[0] for entry in found]
    places = [entry[1:] or None for entry in found]
    width = arrays[0].shape[2]
    length = attended.shape[1]
    smem = pl.BlockSpec(memory_space=pltpu.SMEM)
    vmem = pl.BlockSpec(memory_space=pltpu.VMEM)
    held = [pltpu.VMEM((2, length, width), bf16)] if places[0] else []
    return pl.pallas_call(
        functools.partial(chunk_kernel, places, chunk),
        in_specs=[smem, smem] + [vmem] * (2 + len(arrays)),
        out_specs=[vmem, vmem],
        out_shape=[
            jax.ShapeDtypeStruct((2, width // 2, 2 * HD), bf16),
            jax.ShapeDtypeStruct((2, length, 2 * HD), f32),
        ],
        scratch_shapes=[pltpu.VMEM((2 * HD, width), f32)] + held,
        compiler_params=pltpu.CompilerParams(vmem_limit_bytes=60 * 2**20),
        cost_estimate=pl.CostEstimate(
            flops=7_000_000_000, bytes_accessed=7_000_000, transcendentals=0
        ),
        name="chunk_gradient",
    )(position, scale, attended, out_w.reshape(2, 2, width // 2, 2 * HD), *arrays)


def grad_value_kernel(position, scale, part_0, part_1, normed, probs, grad, total):
    image = pl.program_id(0)
    d_attended = ((part_0[0] + part_1[0]) * scale[image]).astype(bf16)
    d_values = jnp.concatenate(
        [
            lax.dot_general(
                d_attended[:, e * HD : e * HD + HD].T, probs[0, e], (((1,), (0,)), ((), ())),
                preferred_element_type=f32,
            ).astype(bf16)
            for e in range(2)
        ],
        axis=0,
    )
    term = jnp.dot(d_values, normed[0], preferred_element_type=f32)

    @pl.when(image == 0)
    def _():
        total[...] = term

    @pl.when(image == 1)
    def _():
        total[...] += term
        for k in range(NZ):
            part = slice(k * 384, k * 384 + 384)
            store_heads(grad, (), part, position, total[:, part])


def value_gradient(position, scale, *images):
    width = images[2].shape[2]

    def image_spec(a):
        zeros = (0,) * (a.ndim - 1)
        return pl.BlockSpec((1,) + a.shape[1:], lambda i: (i,) + zeros)

    smem = pl.BlockSpec(memory_space=pltpu.SMEM)
    return pl.pallas_call(
        grad_value_kernel,
        grid=(2,),
        in_specs=[smem, smem] + [image_spec(a) for a in images],
        out_specs=pl.BlockSpec((width, 2 * HD), lambda i: (0, 0)),
        out_shape=jax.ShapeDtypeStruct((width, 2 * HD), bf16),
        scratch_shapes=[pltpu.VMEM((2 * HD, width), f32)],
        compiler_params=pltpu.CompilerParams(vmem_limit_bytes=60 * 2**20),
        cost_estimate=pl.CostEstimate(flops=10_000_000_000, bytes_accessed=10_000_000, transcendentals=0),
        name="grad_value",
    )(position, scale, *images)


def start_y(pieces, dp, y_hi, near):
    def piece(mask):
        chosen = lax.dynamic_index_in_dim(pieces, dp ^ (mask >> 1), 0, keepdims=False)
        return lax.dynamic_index_in_dim(chosen, y_hi ^ (mask & 1), 1, keepdims=False)

    return jnp.stack([piece(near), piece(1)]), piece(5 - near), piece(0)


def finish_y(came, kept, near):
    came = came.astype(f32)
    passed = (kept[0].astype(f32) + came[1]).astype(bf16)
    passed = flip(passed, Y, 5 - near, 4).astype(f32)
    return (kept[1].astype(f32) + came[0] + passed).astype(bf16)


def reduce_z(shares, z):
    result = None
    for step in range(NZ):
        piece = lax.dynamic_index_in_dim(shares, (z + step) % NZ, 1, keepdims=False)
        term = (piece if step == 0 else shift(piece, "z", step, NZ)).astype(f32)
        result = term if result is None else result + term
    return result.astype(bf16)


def body(latents, noise, timesteps, ref_errors, norm_gain, w_query, w_key, w_value, w_out):
    dp, z, y_hi = lax.axis_index("dp"), lax.axis_index("z"), lax.axis_index("yh")
    local_len, model_width = latents.shape[1], latents.shape[3]
    full_len = local_len * 8

    def head(weight, which):
        return jnp.where(which == 0, weight[:, :HD], weight[:, HD:])

    def heads(which):
        return jnp.concatenate([head(w, which) for w in (w_query, w_key, w_value, w_out.T)], axis=1)

    position = [z, dp, lax.axis_index("x"), lax.axis_index("core")]
    position = jnp.stack(position).astype(jnp.int32)
    crossed = flip(heads(1 - dp), Y, 3, 4)

    clean32 = latents[0].transpose(1, 0, 2).astype(f32)
    noise32 = noise[0].transpose(1, 0, 2).astype(f32)
    sigma = (timesteps[0].astype(f32) + 0.5) / NSTEP
    mixing = sigma[:, None, None]
    noised = ((1.0 - mixing) * clean32 + mixing * noise32).astype(bf16).astype(f32)
    target = noise32 - clean32
    inverse = lax.rsqrt(jnp.mean(noised * noised, axis=-1, keepdims=True) + norm_epsilon)
    normed = (noised * inverse * norm_gain).astype(bf16)
    normed, crossed = lax.optimization_barrier((normed, crossed))
    own, rest = gather_weight(heads(dp), crossed, y_hi)
    normed = lax.all_gather(normed, SEQ, axis=1, tiled=True)
    attended, probs, partial, out_w = forward(position, normed, own, rest)
    predicted = lax.psum_scatter(partial, SEQ, scatter_dimension=1, tiled=True).astype(f32)
    differ = predicted - target
    residual = differ.astype(bf16)
    sums = jnp.sum(differ * differ, axis=(1, 2))
    sums = sums + flip(sums, "core", 1, 2)
    residual, sums = lax.optimization_barrier((residual, sums))

    def columns(chunk):
        parts = jnp.split(residual, 4, axis=2)
        return jnp.concatenate([parts[chunk], parts[2 + chunk]], axis=2)

    residual_1 = lax.all_gather(columns(1), SEQ, axis=1, tiled=True)
    sums = (sums + flip(sums, "x", 1, 4)) + (flip(sums, "x", 2, 4) + flip(sums, "x", 3, 4))
    sums, own = lax.optimization_barrier((sums, columns(0)))
    found = gather_tokens(own)
    found = [found, [(residual_1,)]]
    errors = sums / (full_len * model_width)
    reference_pair = ref_errors[0]
    margin = errors[0] - reference_pair[0] - (errors[1] - reference_pair[1])
    pair_loss = jax.nn.softplus(preference_beta * margin)
    weight_pair = (
        preference_beta
        * jax.nn.sigmoid(preference_beta * margin)
        * 2.0
        * LOSS_SCALE
        / (full_len * model_width)
    )
    image_scale = jnp.array([1.0, -1.0], f32) * weight_pair

    def first(chunk, scale):
        grad, part = chunk_gradient(chunk, position, scale, attended, out_w, found[chunk])
        send, *kept = start_y(grad.reshape(2, 4, 2, -1, 2 * HD), dp, y_hi, 2 + chunk)
        return part, send, kept

    part_0, send_0, kept_0 = first(0, image_scale)
    send_0, scale_1 = lax.optimization_barrier((send_0, image_scale))
    came_0 = flip(send_0, Y, 2, 4)
    part_1, send_1, kept_1 = first(1, scale_1)
    send_1, scale_2 = lax.optimization_barrier((send_1, scale_1))
    came_1 = flip(send_1, Y, 3, 4)
    grad_value = value_gradient(position, scale_2, part_0, part_1, normed, probs)
    grad_value, came_0, came_1 = lax.optimization_barrier((grad_value, came_0, came_1))
    pieces = grad_value.reshape(2, NZ, 2, -1, 2 * HD)
    value_shares = []
    for half in range(2):
        send, *kept = start_y(pieces[:, 4 * half : 4 * half + 4], dp, y_hi, 2 + half)
        value_shares.append(finish_y(flip(send, Y, 2 + half, 4), kept, 2 + half))
    out_shares = [finish_y(came_0, kept_0, 2), finish_y(came_1, kept_1, 3)]
    shares = jnp.stack([jnp.concatenate(value_shares), jnp.concatenate(out_shares)])
    summed = reduce_z(shares, z)
    return summed[0], summed[1].T, pair_loss.reshape(1)


def solution(mesh):
    fine = Mesh(mesh.devices.reshape(2, NZ, 2, 4, 2), ("dp", "z", "yh", "x", "core"))
    fsdp = ("z", "yh")
    in_specs = (
        P(GROUP, SEQ, None, None),
        P(GROUP, SEQ, None, None),
        P(GROUP, None),
        P(GROUP, None),
        P(),
        P(fsdp, SEQ),
        P(fsdp, SEQ),
        P(fsdp, SEQ),
        P(SEQ, fsdp),
    )
    out_specs = (P(GROUP, SEQ), P(SEQ, GROUP), P(GROUP))
    return jax.shard_map(body, mesh=fine, in_specs=in_specs, out_specs=out_specs, check_vma=False)
```
